512 devices in a mesh: dp: 32 (over z, core), adapter: 16 (over x, y).
Axes of the slice: x: 4, y: 4, z: 16, core: 2. Of those that a mesh axis runs over, the one named last changes fastest.
Arguments:
- activations: bfloat16 [32768, 8192], P('dp', 'adapter'), may hold values from -6 to 6
- cotangent: bfloat16 [32768, 8192], P('dp', 'adapter'), may hold values from -24 to 24
- adapter_down_weights: bfloat16 [64, 8192, 64], P('dp', 'adapter'), may hold values from -0.0625 to 0.0625
- adapter_up_weights: bfloat16 [64, 64, 8192], P('dp', None, 'adapter'), may hold values from -0.125 to 0.125
- adapter_of_block: int32 [256], replicated, may hold values from 0 to 63, as said below
Outputs:
- adapter_branch_output: bfloat16 [32768, 8192], P('dp', 'adapter')
- input_grad: bfloat16 [32768, 8192], P('dp', 'adapter')
- down_grad: float32 [64, 8192, 64], P('dp', 'adapter')
- up_grad: float32 [64, 64, 8192], P('dp', None, 'adapter')
The draws below stay inside these ranges and needn't reach their ends.
Inputs may be any that keep to these rules, and one draw needn't show every extreme that they name: `adapter_of_block`: the blocks 8 * p to 8 * p + 8 - 1 (those of index p of dp) name adapters of distinct owners, where the owner of adapter a is a // 2. Every adapter is named by some block, and some owner is named by a block of every index of dp.
All inputs are finite; a program needn't handle non-finite values.
Results may differ from the reference program's by a relative error of at most 0.0049.
Values may be sent and summed in bfloat16 or wider, within the bound.
No kernel may reach another device: no remote copies, remote signals or barrier semaphores. Data moves between devices by JAX's collectives and lax.ppermute only.
A program may use at most 64 MiB of HBM per device.

```python
import jax
import jax.numpy as jnp
from jax import lax

MODEL_WIDTH = 8192
ADAPTER_RANK = 64
BLOCK = 128
ADP_DEV = 2
BLK_DEV = 8
NBLK = 256
TOKENS = 32768
ADAPTER_TOTAL = 64
N_DP = 32


def draw_adapter_of_block(key, part):
    key = jax.random.fold_in(key, 11)
    sorting_keys = jax.random.split(key, 5)
    offset = jax.random.randint(sorting_keys[0], (), 0, N_DP)
    sources = jnp.arange(N_DP, dtype=jnp.int32)
    first_owner = (sources + offset) % N_DP
    second_owner = (sources + offset + N_DP // 2) % N_DP
    ordering_list = jax.random.permutation(sorting_keys[1], N_DP).astype(jnp.int32)
    extra_term = ordering_list * 2048 + jnp.where(ordering_list == N_DP - 1, 4194304, 0)
    score_values = jax.random.randint(sorting_keys[2], (N_DP, N_DP), 0, 65536) + extra_term[None, :]
    owners_all = jnp.arange(N_DP, dtype=jnp.int32)[None, :]
    taken = (owners_all == first_owner[:, None]) | (owners_all == second_owner[:, None])
    score_values = jnp.where(taken, -1, score_values) * 64 + owners_all
    picked = lax.top_k(score_values, BLK_DEV - 2)[1].astype(jnp.int32)
    parity = jax.random.randint(sorting_keys[3], (N_DP, BLK_DEV - 2), 0, 2)
    owners = jnp.concatenate([first_owner[:, None], second_owner[:, None], picked], axis=1)
    bits = jnp.concatenate([jnp.zeros((N_DP, 1), jnp.int32), jnp.ones((N_DP, 1), jnp.int32), parity], axis=1)
    chosen = owners * ADP_DEV + bits
    order_keys = jax.random.randint(sorting_keys[4], (N_DP, BLK_DEV), 0, 1048576) * 64 + jnp.arange(BLK_DEV, dtype=jnp.int32)[None, :]
    order = jnp.argsort(order_keys, axis=1)
    chosen = jnp.take_along_axis(chosen, order, axis=1)
    return chosen.reshape(N_DP * BLK_DEV).astype(jnp.int32)


def block_scale(rng, shape, cuts, low, top_value):
    loudness, own = 1.0, jax.random.fold_in(rng, 6)
    for dim, blocks in cuts:
        steps = jnp.exp(jax.random.uniform(jax.random.fold_in(own, dim), (blocks,), jnp.float32, low / len(cuts), top_value / len(cuts)))
        loudness = loudness * jnp.repeat(steps, shape[dim] // blocks).reshape([-1 if axis == dim else 1 for axis in range(len(shape))])
    return loudness


def noise(own_key, dims, scale, bound, pieces=(), kind=jnp.bfloat16):
    drawn = scale * jax.random.normal(own_key, dims, jnp.float32)
    if pieces:
        drawn = drawn * block_scale(own_key, dims, pieces, -0.22, 0.18)
    return jnp.clip(drawn, -bound, bound).astype(kind)


def setup_inputs(seed: int = 0) -> dict:
    splits = jax.random.split(jax.random.key(seed), 6)
    return {
        "activations": noise(splits[0], (TOKENS, MODEL_WIDTH), 1.0, 6.0, ((0, 32), (1, 16))),
        "cotangent": noise(splits[1], (TOKENS, MODEL_WIDTH), 4.0, 24.0, ((0, 32), (1, 16))),
        "adapter_down_weights": noise(splits[2], (ADAPTER_TOTAL, MODEL_WIDTH, ADAPTER_RANK), MODEL_WIDTH ** -0.5, 0.0625, ((0, 32), (1, 16))),
        "adapter_up_weights": noise(splits[3], (ADAPTER_TOTAL, ADAPTER_RANK, MODEL_WIDTH), (MODEL_WIDTH // 4) ** -0.5, 0.125, ((0, 32), (2, 16))),
        "adapter_of_block": draw_adapter_of_block(jax.random.fold_in(splits[5], 71), 0),
    }


adapter_scale = 2.0


def reference(activations, cotangent, adapter_down_weights, adapter_up_weights, adapter_of_block):
    blocks_in = activations.reshape(NBLK, BLOCK, MODEL_WIDTH)
    blocks_co = cotangent.reshape(NBLK, BLOCK, MODEL_WIDTH)

    def per_block(item):
        rows_in, rows_companion, selected_adapter = item
        down_matrix = adapter_down_weights[selected_adapter]
        upper_limit = adapter_up_weights[selected_adapter]
        projected_rows = jnp.dot(rows_in, down_matrix, preferred_element_type=jnp.float32).astype(jnp.bfloat16)
        output_rows = (adapter_scale * jnp.dot(projected_rows, upper_limit, preferred_element_type=jnp.float32)).astype(jnp.bfloat16)
        backward_result = (adapter_scale * jnp.dot(rows_companion, upper_limit.T, preferred_element_type=jnp.float32)).astype(jnp.bfloat16)
        grad_rows = jnp.dot(backward_result, down_matrix.T, preferred_element_type=jnp.float32).astype(jnp.bfloat16)
        down_part = jnp.dot(rows_in.T, backward_result, preferred_element_type=jnp.float32).astype(jnp.bfloat16)
        up_piece = (adapter_scale * jnp.dot(projected_rows.T, rows_companion, preferred_element_type=jnp.float32)).astype(jnp.bfloat16)
        return output_rows, grad_rows, down_part, up_piece

    outputs, grads, down_parts, up_parts = lax.map(per_block, (blocks_in, blocks_co, adapter_of_block))
    counts = jnp.sum((adapter_of_block[:, None] == jnp.arange(ADAPTER_TOTAL, dtype=jnp.int32)[None, :]).astype(jnp.float32), axis=0) * BLOCK
    down_grad = jax.ops.segment_sum(down_parts.astype(jnp.float32), adapter_of_block, ADAPTER_TOTAL) / counts[:, None, None]
    up_grad = jax.ops.segment_sum(up_parts.astype(jnp.float32), adapter_of_block, ADAPTER_TOTAL) / counts[:, None, None]
    return outputs.reshape(TOKENS, MODEL_WIDTH), grads.reshape(TOKENS, MODEL_WIDTH), down_grad, up_grad
```

```python
import jax
import jax.numpy as jnp
from jax import lax
from jax.experimental import pallas as pl
from jax.experimental.pallas import tpu as pltpu
from jax.sharding import Mesh, PartitionSpec as P

BLOCK = 128
SCALE = 2.0
CORES = 2
PIECE = (16, 128)
F32, BF16 = jnp.float32, jnp.bfloat16

VMEM = pl.BlockSpec(memory_space=pltpu.VMEM)
SMEM = pl.BlockSpec(memory_space=pltpu.SMEM)
ANY = pl.BlockSpec(memory_space=pl.ANY)
NT = (((1,), (1,)), ((), ()))
NN = (((1,), (0,)), ((), ()))
TN = (((0,), (0,)), ((), ()))


def dot(a, b, dims):
    return lax.dot_general(a, b, dims, preferred_element_type=F32)


def call(body, outs, ins, in_specs, scratch=(), out_specs=None):
    return pl.pallas_call(
        body,
        out_shape=outs,
        in_specs=in_specs,
        out_specs=out_specs or jax.tree.map(lambda _: VMEM, outs),
        scratch_shapes=list(scratch),
        compiler_params=pltpu.CompilerParams(vmem_limit_bytes=40 * 2**20),
    )(*ins)


def shape(dims, kind):
    return jax.ShapeDtypeStruct(dims, kind)


def named(table, where, dev_z, core, block, blocks):
    adapter = table[(dev_z * CORES + core) * blocks + block]
    owner = adapter // 2
    return owner % 2, (owner // 2) * 2 + adapter % 2


def pick_pieces(table, where, mine, other, out):
    nz, blocks = out.shape[0], out.shape[1]
    core = where[1]

    def step(i, _):
        z, b = i // blocks, i % blocks
        par, row = named(table, where, z, core, b, blocks)
        out[z, b] = jnp.where(par == core, mine[row], other[row])
        return 0

    lax.fori_loop(0, nz * blocks, step, 0, unroll=8)


def assemble(pieces, b, per_row):
    rows = []
    for i in range(pieces.shape[0] // per_row):
        rows.append(jnp.concatenate([pieces[i * per_row + j, b] for j in range(per_row)], axis=1))
    return jnp.concatenate(rows, axis=0)


def pad_low(w):
    return jnp.concatenate([w, jnp.zeros_like(w)], axis=0)


def pad_high(w):
    return jnp.concatenate([jnp.zeros_like(w), w], axis=0)


def rows_of(ref, b):
    return ref[b * BLOCK:(b + 1) * BLOCK, :]


def back_partial(cot, pieces, out):
    half = pieces.shape[1] // 2
    per_row = cot.shape[1] // PIECE[1]
    for j in range(half):
        low = dot(rows_of(cot, j), pad_low(assemble(pieces, j, per_row)), NT)
        high = dot(rows_of(cot, j + half), pad_high(assemble(pieces, j + half, per_row)), NT)
        out[j * BLOCK:(j + 1) * BLOCK, :] = SCALE * (low + high)


def grads_down(acts, back, out):
    half = out.shape[0] // 2
    rank = out.shape[1]
    for j in range(half):
        b = rows_of(back, j)
        out[j] = dot(b, rows_of(acts, j), TN)[:rank].astype(BF16)
        out[j + half] = dot(b, rows_of(acts, j + half), TN)[rank:].astype(BF16)


def grads_up(cot, proj, out):
    half = out.shape[1] // 2
    per_row = cot.shape[1] // PIECE[1]
    rank = out.shape[0] // per_row * PIECE[0]

    def put(b, g):
        g = (SCALE * g).astype(BF16)
        for i in range(rank // PIECE[0]):
            for j in range(per_row):
                out[i * per_row + j, b] = g[i * PIECE[0]:(i + 1) * PIECE[0], j * PIECE[1]:(j + 1) * PIECE[1]]

    for j in range(half):
        p = rows_of(proj, j)
        put(j, dot(p, rows_of(cot, j), TN)[:rank])
        put(j + half, dot(p, rows_of(cot, j + half), TN)[rank:])


def sum_pieces(table, where, got, keep, send, acc):
    nz, blocks = got.shape[0], got.shape[1]
    core = where[1]
    half = keep.shape[0]
    acc[...] = jnp.zeros_like(acc)

    def step(i, _):
        z, b = i // blocks, i % blocks
        par, row = named(table, where, z, core, b, blocks)
        at = par * half + row
        acc[at] = acc[at] + got[z, b].astype(F32)
        return 0

    lax.fori_loop(0, nz * blocks, step, 0, unroll=8)
    keep[...] = acc[pl.ds(core * half, half)]
    send[...] = acc[pl.ds((1 - core) * half, half)]


def pick_for_other(table, where, gathered, out, sems):
    blocks = out.shape[0]
    copies = []
    for b in range(blocks):
        _, row = named(table, where, where[0], 1 - where[1], b, blocks)
        copies.append(pltpu.make_async_copy(gathered.at[row], out.at[b], sems.at[b]))
    for c in copies:
        c.start()
    for c in copies:
        c.wait()


def proj_partial(table, where, acts, gathered, other, out, chosen, sems):
    blocks = chosen.shape[0]
    half = blocks // 2
    core = where[1]
    copies, pars = [], []
    for b in range(blocks):
        par, row = named(table, where, where[0], core, b, blocks)
        copies.append(pltpu.make_async_copy(gathered.at[row], chosen.at[b], sems.at[b]))
        pars.append(par)
    for c in copies:
        c.start()
    for b in range(blocks):
        copies[b].wait()
        chosen[b] = jnp.where(pars[b] == core, chosen[b], other[b])
    for j in range(half):
        low = dot(rows_of(acts, j), pad_low(chosen[j]), NT)
        high = dot(rows_of(acts, j + half), pad_high(chosen[j + half]), NT)
        out[j * BLOCK:(j + 1) * BLOCK, :] = low + high


def place_parts(table, where, mine, other, out):
    blocks = mine.shape[0]
    core = where[1]
    out[...] = jnp.zeros_like(out)
    for b in range(blocks):
        par, row = named(table, where, where[0], core, b, blocks)

        @pl.when(par == core)
        def _():
            out[row] = mine[b]

    for b in range(blocks):
        par, row = named(table, where, where[0], 1 - core, b, blocks)

        @pl.when(par == core)
        def _():
            out[row] = (out[row].astype(F32) + other[b].astype(F32)).astype(BF16)


def outputs(proj, back, pieces, chosen, out, grad):
    half = chosen.shape[0] // 2
    per_row = out.shape[1] // PIECE[1]
    for b in range(2 * half):
        pad = pad_low if b < half else pad_high
        p, k = rows_of(proj, b % half), rows_of(back, b % half)
        out[b * BLOCK:(b + 1) * BLOCK, :] = (SCALE * dot(p, pad(assemble(pieces, b, per_row)), NN)).astype(BF16)
        grad[b * BLOCK:(b + 1) * BLOCK, :] = dot(k, pad(chosen[b]), NN).astype(BF16)


def local(activations, cotangent, adapter_down_weights, adapter_up_weights, table):
    nz, nxy = lax.axis_size("z"), lax.axis_size("xy")
    share, width, rank = adapter_down_weights.shape
    tokens = activations.shape[0]
    blocks = tokens // BLOCK
    across, along = rank // PIECE[0], width // PIECE[1]
    where = jnp.stack([lax.axis_index("z"), lax.axis_index("core")]).astype(jnp.int32)
    swap = [(0, 1), (1, 0)]
    own = nz * share

    def over_z(x):
        return lax.all_to_all(x, "z", 0, 0, tiled=True)

    def total(part):
        rows = part.shape[0] // nxy
        got = lax.all_to_all(part.reshape(nxy, rows, part.shape[1]), "xy", 0, 0, tiled=True)
        mine = jnp.sum(got, axis=0).astype(BF16)
        spread = jnp.broadcast_to(mine[None], (nxy,) + mine.shape)
        return lax.all_to_all(spread, "xy", 0, 0, tiled=True).reshape(part.shape)

    gathered = lax.all_gather(jnp.swapaxes(adapter_down_weights, 1, 2), "z", tiled=True)

    cut = adapter_up_weights.reshape(share, across, PIECE[0], along, PIECE[1])
    cut = cut.transpose(1, 3, 0, 2, 4).reshape(nz, share, *PIECE)
    held = over_z(cut).reshape(own, *PIECE)
    held_other = lax.ppermute(held, "core", swap)
    wanted = call(pick_pieces, shape((nz, blocks) + PIECE, BF16), (table, where, held, held_other), [SMEM, SMEM, VMEM, VMEM])
    pieces = over_z(wanted)
    back = total(call(back_partial, shape((tokens // 2, 2 * rank), F32), (cotangent, pieces), [VMEM, VMEM]))

    part_down = call(grads_down, shape((blocks, rank, width), BF16), (activations, back), [VMEM, VMEM])
    part_other = lax.ppermute(part_down, "core", swap)
    placed = call(place_parts, shape((own, rank, width), BF16), (table, where, part_down, part_other), [SMEM, SMEM, VMEM, VMEM])
    summed = lax.psum_scatter(placed, "z", scatter_dimension=0, tiled=True)

    gathered, _ = lax.optimization_barrier((gathered, back))
    for_other = call(
        pick_for_other, shape((blocks, rank, width), BF16), (table, where, gathered), [SMEM, SMEM, ANY],
        [pltpu.SemaphoreType.DMA((blocks,))],
    )
    from_other = lax.ppermute(for_other, "core", swap)
    proj_part, chosen = call(
        proj_partial,
        (shape((tokens // 2, 2 * rank), F32), shape((blocks, rank, width), BF16)),
        (table, where, activations, gathered, from_other),
        [SMEM, SMEM, VMEM, ANY, VMEM],
        [pltpu.SemaphoreType.DMA((blocks,))],
    )
    proj = total(proj_part)
    part_up = call(grads_up, shape((nz, blocks) + PIECE, BF16), (cotangent, proj), [VMEM, VMEM])
    got = over_z(part_up)
    keep, send = call(
        sum_pieces, (shape((own,) + PIECE, F32),) * 2, (table, where, got), [SMEM, SMEM, VMEM],
        [pltpu.VMEM((CORES * own,) + PIECE, F32)],
    )
    merged = (keep + lax.ppermute(send, "core", swap)).astype(BF16)
    owned = over_z(merged.reshape(nz, share, *PIECE))

    out, grad = call(
        outputs, (shape((tokens, width), BF16),) * 2, (proj, back, pieces, chosen), [VMEM] * 4,
    )

    ids = (where[0] * CORES + where[1]) * share + jnp.arange(share, dtype=jnp.int32)
    counts = jnp.sum((table[:, None] == ids[None, :]).astype(F32), axis=0) * BLOCK
    counts = counts[:, None, None]
    down_grad = jnp.swapaxes(summed.astype(F32) / counts, 1, 2)
    up_grad = owned.reshape(across, along, share, *PIECE).transpose(2, 0, 3, 1, 4)
    up_grad = up_grad.reshape(share, rank, width).astype(F32) / counts
    return out, grad, down_grad, up_grad


def solution(mesh):
    nxy = mesh.shape["adapter"]
    grid = Mesh(mesh.devices.reshape(-1, CORES, nxy), ("z", "core", "xy"))
    dp = ("z", "core")
    specs = (P(dp, "xy"), P(dp, "xy"), P(dp, "xy", None), P(dp, None, "xy"))
    return jax.shard_map(
        local, mesh=grid, in_specs=specs + (P(),), out_specs=specs, check_vma=False
    )
```

```python
import jax
import jax.numpy as jnp
from jax import lax
from jax.experimental import pallas as pl
from jax.experimental.pallas import tpu as pltpu
from jax.sharding import Mesh, PartitionSpec as P

BLOCK = 128
SCALE = 2.0
CORES = 2
HALF = 16
PIECE = (2 * HALF, 128)
F32, BF16 = jnp.float32, jnp.bfloat16

VMEM = pl.BlockSpec(memory_space=pltpu.VMEM)
SMEM = pl.BlockSpec(memory_space=pltpu.SMEM)
NT = (((1,), (1,)), ((), ()))
NN = (((1,), (0,)), ((), ()))
TN = (((0,), (0,)), ((), ()))


def dot(a, b, dims):
    return lax.dot_general(a, b, dims, preferred_element_type=F32)


def call(body, outs, ins, in_specs, scratch=()):
    return pl.pallas_call(
        body,
        out_shape=outs,
        in_specs=in_specs,
        out_specs=jax.tree.map(lambda _: VMEM, outs),
        scratch_shapes=list(scratch),
        compiler_params=pltpu.CompilerParams(vmem_limit_bytes=40 * 2**20),
    )(*ins)


def shape(dims, kind):
    return jax.ShapeDtypeStruct(dims, kind)


def named(table, z, core, block, blocks):
    adapter = table[(z * CORES + core) * blocks + block]
    owner = adapter // 2
    return owner % 2, (owner // 2) * 2 + adapter % 2


def pieces_of(matrix):
    across, along = matrix[0] // HALF, matrix[1] // PIECE[1]
    for i in range(across):
        for j in range(along):
            yield i * along + j, slice(i * HALF, (i + 1) * HALF), slice(j * PIECE[1], (j + 1) * PIECE[1])


def cut(down, up, out):
    for k in range(down.shape[0]):
        for h, r, c in pieces_of(down.shape[1:]):
            out[h, k, :HALF] = down[k, r, c]
            out[h, k, HALF:] = up[k, r, c]


def means(counts, owned, down, up):
    for k in range(down.shape[0]):
        for h, r, c in pieces_of(down.shape[1:]):
            mean = owned[h, k].astype(F32) / counts[k]
            down[k, r, c] = mean[:HALF]
            up[k, r, c] = mean[HALF:]


def pick_pieces(table, where, mine, other, out, held):
    nz, blocks = out.shape[0], out.shape[1]
    half = mine.shape[0]
    core = where[1]
    held[:half] = mine[...]
    held[half:] = other[...]

    def step(z, _):
        for b in range(blocks):
            par, row = named(table, z, core, b, blocks)
            out[z, b] = held[jnp.where(par == core, row, row + half)]
        return 0

    lax.fori_loop(0, nz, step, 0, unroll=2)


def assemble(pieces, b, which, per_row):
    rows = []
    for i in range(pieces.shape[0] // per_row):
        parts = [pieces[i * per_row + j, b, which * HALF:(which + 1) * HALF] for j in range(per_row)]
        rows.append(jnp.concatenate(parts, axis=1))
    return jnp.concatenate(rows, axis=0)


def low(w):
    return jnp.concatenate([w, jnp.zeros_like(w)], axis=0)


def high(w):
    return jnp.concatenate([jnp.zeros_like(w), w], axis=0)


def rows_of(ref, b):
    return ref[b * BLOCK:(b + 1) * BLOCK, :]


def partial_sums(acts, cot, pieces, out):
    per_row = acts.shape[1] // PIECE[1]
    for b in range(pieces.shape[1]):
        proj = dot(rows_of(acts, b), low(assemble(pieces, b, 0, per_row)), NT)
        back = dot(rows_of(cot, b), high(assemble(pieces, b, 1, per_row)), NT)
        out[b * BLOCK:(b + 1) * BLOCK, :] = proj + SCALE * back


def block_grads(acts, cot, sums, out):
    rank = sums.shape[1] // 2
    for b in range(out.shape[1]):
        p = rows_of(sums, b)
        down = dot(p, rows_of(acts, b), TN)[rank:].astype(BF16)
        up = (SCALE * dot(p, rows_of(cot, b), TN)[:rank]).astype(BF16)
        for which, g in enumerate((down, up)):
            for h, r, c in pieces_of(g.shape):
                out[h, b, which * HALF:(which + 1) * HALF] = g[r, c]


def sum_pieces(table, where, got, keep, send, acc):
    nz, blocks = got.shape[0], got.shape[1]
    core = where[1]
    half = keep.shape[0]
    acc[...] = jnp.zeros_like(acc)

    def step(z, _):
        for b in range(blocks):
            par, row = named(table, z, core, b, blocks)
            at = par * half + row
            acc[at] = acc[at] + got[z, b].astype(F32)
        return 0

    lax.fori_loop(0, nz, step, 0, unroll=2)
    keep[...] = acc[pl.ds(core * half, half)]
    send[...] = acc[pl.ds((1 - core) * half, half)]


def outputs(sums, pieces, out, grad):
    per_row = out.shape[1] // PIECE[1]
    for b in range(pieces.shape[1]):
        p = rows_of(sums, b)
        at = slice(b * BLOCK, (b + 1) * BLOCK)
        out[at, :] = (SCALE * dot(p, low(assemble(pieces, b, 1, per_row)), NN)).astype(BF16)
        grad[at, :] = dot(p, high(assemble(pieces, b, 0, per_row)), NN).astype(BF16)


def local(activations, cotangent, adapter_down_weights, adapter_up_weights, table):
    nz, nxy = lax.axis_size("z"), lax.axis_size("xy")
    share, width, rank = adapter_down_weights.shape
    tokens = activations.shape[0]
    blocks = tokens // BLOCK
    where = jnp.stack([lax.axis_index("z"), lax.axis_index("core")]).astype(jnp.int32)
    swap = [(0, 1), (1, 0)]
    own = nz * share

    def over_z(x):
        return lax.all_to_all(x, "z", 0, 0, tiled=True)

    def total(part):
        rows = part.shape[0] // nxy
        got = lax.all_to_all(part.reshape(nxy, rows, part.shape[1]), "xy", 0, 0, tiled=True)
        mine = jnp.sum(got, axis=0).astype(BF16)
        spread = jnp.broadcast_to(mine[None], (nxy,) + mine.shape)
        return lax.all_to_all(spread, "xy", 0, 0, tiled=True).reshape(part.shape)

    down = jnp.swapaxes(adapter_down_weights, 1, 2)
    pieces = call(cut, shape((nz, share) + PIECE, BF16), (down, adapter_up_weights), [VMEM] * 2)
    held = over_z(pieces).reshape(own, *PIECE)
    held_other = lax.ppermute(held, "core", swap)
    wanted = call(
        pick_pieces, shape((nz, blocks) + PIECE, BF16), (table, where, held, held_other), [SMEM, SMEM, VMEM, VMEM],
        [pltpu.VMEM((CORES * own,) + PIECE, BF16)],
    )
    pieces = over_z(wanted)
    sums = total(
        call(partial_sums, shape((tokens, 2 * rank), F32), (activations, cotangent, pieces), [VMEM] * 3)
    )
    parts = call(
        block_grads, shape((nz, blocks) + PIECE, BF16), (activations, cotangent, sums), [VMEM] * 3
    )
    got = over_z(parts)
    keep, send = call(
        sum_pieces, (shape((own,) + PIECE, F32),) * 2, (table, where, got), [SMEM, SMEM, VMEM],
        [pltpu.VMEM((CORES * own,) + PIECE, F32)],
    )
    merged = (keep + lax.ppermute(send, "core", swap)).astype(BF16)
    owned = over_z(merged.reshape(nz, share, *PIECE))

    out, grad = call(outputs, (shape((tokens, width), BF16),) * 2, (sums, pieces), [VMEM] * 2)

    ids = (where[0] * CORES + where[1]) * share + jnp.arange(share, dtype=jnp.int32)
    counts = jnp.sum((table[:, None] == ids[None, :]).astype(F32), axis=0) * BLOCK
    down_grad, up_grad = call(means, (shape((share, rank, width), F32),) * 2, (counts, owned), [SMEM, VMEM])
    return out, grad, jnp.swapaxes(down_grad, 1, 2), up_grad


def solution(mesh):
    nxy = mesh.shape["adapter"]
    grid = Mesh(mesh.devices.reshape(-1, CORES, nxy), ("z", "core", "xy"))
    dp = ("z", "core")
    specs = (P(dp, "xy"), P(dp, "xy"), P(dp, "xy", None), P(dp, None, "xy"))
    return jax.shard_map(
        local, mesh=grid, in_specs=specs + (P(),), out_specs=specs, check_vma=False
    )
```

```python
import functools

import jax
import jax.numpy as jnp
from jax import lax
from jax.experimental import pallas as pl
from jax.experimental.pallas import tpu as pltpu
from jax.sharding import Mesh, PartitionSpec as P

BLOCK = 128
SCALE = 2.0
CORES = 2
COPIES = 2
GROUP = 8
STEPS = (0, 4, 1, -1, 2, -2, 3, -3)
F32, BF16 = jnp.float32, jnp.bfloat16

VMEM = pl.BlockSpec(memory_space=pltpu.VMEM)
SMEM = pl.BlockSpec(memory_space=pltpu.SMEM)
NT = (((1,), (1,)), ((), ()))
NN = (((1,), (0,)), ((), ()))
TN = (((0,), (0,)), ((), ()))


def dot(a, b, dims):
    return lax.dot_general(a, b, dims, preferred_element_type=F32)


def call(body, outs, ins, in_specs, scratch=()):
    return pl.pallas_call(
        body,
        out_shape=outs,
        in_specs=in_specs,
        out_specs=jax.tree.map(lambda _: VMEM, outs),
        scratch_shapes=list(scratch),
        compiler_params=pltpu.CompilerParams(vmem_limit_bytes=40 * 2**20),
    )(*ins)


def shape(dims, kind):
    return jax.ShapeDtypeStruct(dims, kind)


def named(table, z, core, block, blocks):
    adapter = table[(z * CORES + core) * blocks + block]
    owner = adapter // 2
    return owner % 2, (owner // 2) * 2 + adapter % 2


def cut(down, up, out):
    parts = out.shape[0] // COPIES
    for k in range(down.shape[0]):
        d, u = down[k].astype(F32), up[k].astype(F32)
        for i in range(parts):
            at = slice(i * GROUP, (i + 1) * GROUP)
            piece = jnp.concatenate([d[at], u[at]], axis=0).astype(BF16)
            for copy in range(COPIES):
                out[copy * parts + i, k] = piece


def means(counts, owned, down, up):
    parts = owned.shape[0] // COPIES
    for k in range(down.shape[0]):
        for i in range(parts):
            piece = owned[i, k].astype(F32)
            for copy in range(1, COPIES):
                piece = piece + owned[copy * parts + i, k].astype(F32)
            piece = piece / counts[k]
            down[k, i * GROUP:(i + 1) * GROUP] = piece[:GROUP]
            up[k, i * GROUP:(i + 1) * GROUP] = piece[GROUP:]


def partner(where, nz, step):
    return lax.rem(where[0] + (1 - 2 * where[1]) * step + nz, nz)


def pick_pieces(nz, table, where, mine, other, *outs):
    core = where[1]
    blocks = outs[0].shape[0]
    for step, out in zip(STEPS, outs):
        z = partner(where, nz, step)
        for b in range(blocks):
            par, row = named(table, z, core, b, blocks)

            @pl.when(par == core)
            def _():
                out[b] = mine[row]

            @pl.when(par != core)
            def _():
                out[b] = other[row]


def is_first(dims, axis):
    return lax.broadcasted_iota(jnp.int32, dims, axis) % (2 * GROUP) < GROUP


def rows_of(ref, b):
    return ref[b * BLOCK:(b + 1) * BLOCK, :]


def matrix(pieces, b):
    return jnp.concatenate([p[b] for p in pieces], axis=0)


def partial_sums(acts, cot, *refs):
    pieces, out = refs[:-1], refs[-1]
    lanes = out.shape[1]
    first = is_first((BLOCK, lanes), 1)
    for b in range(pieces[0].shape[0]):
        w = matrix(pieces, b)
        proj, back = dot(rows_of(acts, b), w, NT), dot(rows_of(cot, b), w, NT)
        out[b * BLOCK:(b + 1) * BLOCK, :] = jnp.where(first, proj, SCALE * back)


def swapped(sums, b):
    lanes = sums.shape[1]
    row = lax.broadcasted_iota(jnp.int32, (lanes, lanes), 0)
    col = lax.broadcasted_iota(jnp.int32, (lanes, lanes), 1)
    place = row == jnp.where(is_first((lanes, lanes), 1), col + GROUP, col - GROUP)
    return dot(rows_of(sums, b), place.astype(BF16), NN).astype(BF16)


def block_grads(acts, cot, sums, *outs):
    lanes = sums.shape[1]
    first = is_first((lanes, acts.shape[1]), 0)
    for b in range(outs[0].shape[0]):
        q = swapped(sums, b)
        down, up = dot(q, rows_of(acts, b), TN), dot(q, rows_of(cot, b), TN)
        g = jnp.where(first, down, SCALE * up).astype(BF16)
        for i, out in enumerate(outs):
            out[b] = g[i * 2 * GROUP:(i + 1) * 2 * GROUP]


def outputs(sums, *refs):
    pieces, out, grad = refs[:-2], refs[-2], refs[-1]
    first = is_first((BLOCK, sums.shape[1]), 1)
    for b in range(pieces[0].shape[0]):
        q, w = swapped(sums, b), matrix(pieces, b)
        zero = jnp.zeros_like(q)
        at = slice(b * BLOCK, (b + 1) * BLOCK)
        out[at, :] = (SCALE * dot(jnp.where(first, zero, q), w, NN)).astype(BF16)
        grad[at, :] = dot(jnp.where(first, q, zero), w, NN).astype(BF16)


def sum_pieces(nz, table, where, *refs):
    gots, (keep, send, acc) = refs[:-3], refs[-3:]
    core = where[1]
    half = keep.shape[0]
    blocks = gots[0].shape[0]
    acc[...] = jnp.zeros_like(acc)
    for step, got in zip(STEPS, gots):
        z = partner(where, nz, step)
        for b in range(blocks):
            par, row = named(table, z, core, b, blocks)
            at = par * half + row
            acc[at] = acc[at] + got[b].astype(F32)
    keep[...] = acc[pl.ds(core * half, half)]
    send[...] = acc[pl.ds((1 - core) * half, half)].astype(BF16)


def local(activations, cotangent, adapter_down_weights, adapter_up_weights, table):
    nz, nxy = lax.axis_size("z"), lax.axis_size("xy")
    share, width, rank = adapter_down_weights.shape
    tokens = activations.shape[0]
    blocks = tokens // BLOCK
    piece = (2 * GROUP, width)
    where = jnp.stack([lax.axis_index("z"), lax.axis_index("core")]).astype(jnp.int32)
    swap = [(0, 1), (1, 0)]
    own = nz * share
    slots = (shape((blocks,) + piece, BF16),) * len(STEPS)

    def over_z(x):
        return lax.all_to_all(x, "z", 0, 0, tiled=True)

    def shift(x, step):
        if step == 0:
            return x
        pairs = [(z * CORES + c, (z + (step, -step)[c]) % nz * CORES + c) for z in range(nz) for c in range(CORES)]
        return lax.ppermute(x, ("z", "core"), pairs)

    def total(part):
        rows = part.shape[0] // nxy
        got = lax.all_to_all(part.reshape(nxy, rows, part.shape[1]), "xy", 0, 0, tiled=True)
        mine = jnp.sum(got, axis=0).astype(BF16)
        spread = jnp.broadcast_to(mine[None], (nxy,) + mine.shape)
        return lax.all_to_all(spread, "xy", 0, 0, tiled=True).reshape(part.shape)

    down = jnp.swapaxes(adapter_down_weights, 1, 2)
    spread = call(cut, shape((nz, share) + piece, BF16), (down, adapter_up_weights), [VMEM] * 2)
    held = over_z(spread).reshape(own, *piece)
    held_other = lax.ppermute(held, "core", swap)
    wanted = call(
        functools.partial(pick_pieces, nz), slots, (table, where, held, held_other), [SMEM, SMEM, VMEM, VMEM]
    )
    pieces = [shift(w, step) for w, step in zip(wanted, STEPS)]
    sums = total(
        call(
            partial_sums, shape((tokens, 2 * rank), F32), (activations, cotangent, *pieces), [VMEM] * (2 + len(STEPS))
        )
    )
    parts = call(block_grads, slots, (activations, cotangent, sums), [VMEM] * 3)
    gots = [shift(g, -step) for g, step in zip(parts, STEPS)]
    keep, send = call(
        functools.partial(sum_pieces, nz), (shape((own,) + piece, F32), shape((own,) + piece, BF16)),
        (table, where, *gots), [SMEM, SMEM] + [VMEM] * len(STEPS), [pltpu.VMEM((CORES * own,) + piece, F32)],
    )
    merged = (keep + lax.ppermute(send, "core", swap).astype(F32)).astype(BF16)
    owned = over_z(merged.reshape(nz, share, *piece))

    out, grad = call(outputs, (shape((tokens, width), BF16),) * 2, (sums, *pieces), [VMEM] * (1 + len(STEPS)))

    ids = (where[0] * CORES + where[1]) * share + jnp.arange(share, dtype=jnp.int32)
    counts = jnp.sum((table[:, None] == ids[None, :]).astype(F32), axis=0) * BLOCK
    down_grad, up_grad = call(means, (shape((share, rank, width), F32),) * 2, (counts, owned), [SMEM, VMEM])
    return out, grad, jnp.swapaxes(down_grad, 1, 2), up_grad


def solution(mesh):
    nxy = mesh.shape["adapter"]
    grid = Mesh(mesh.devices.reshape(-1, CORES, nxy), ("z", "core", "xy"))
    dp = ("z", "core")
    specs = (P(dp, "xy"), P(dp, "xy"), P(dp, "xy", None), P(dp, None, "xy"))
    return jax.shard_map(
        local, mesh=grid, in_specs=specs + (P(),), out_specs=specs, check_vma=False
    )
```

```python
import functools

import jax
import jax.numpy as jnp
from jax import lax
from jax.experimental import pallas as pl
from jax.experimental.pallas import tpu as pltpu
from jax.sharding import Mesh, PartitionSpec as P

BLOCK = 128
SCALE = 2.0
CORES = 2
COPIES = 2
GROUP = 8
STEPS = (0, 4, 1, -1, 2, -2, 3, -3)
F32, BF16 = jnp.float32, jnp.bfloat16

VMEM = pl.BlockSpec(memory_space=pltpu.VMEM)
SMEM = pl.BlockSpec(memory_space=pltpu.SMEM)
NT = (((1,), (1,)), ((), ()))
NN = (((1,), (0,)), ((), ()))
TN = (((0,), (0,)), ((), ()))


def dot(a, b, dims):
    return lax.dot_general(a, b, dims, preferred_element_type=F32)


def call(body, outs, ins, in_specs, scratch=()):
    return pl.pallas_call(
        body,
        out_shape=outs,
        in_specs=in_specs,
        out_specs=jax.tree.map(lambda _: VMEM, outs),
        scratch_shapes=list(scratch),
        compiler_params=pltpu.CompilerParams(vmem_limit_bytes=40 * 2**20),
    )(*ins)


def shape(dims, kind):
    return jax.ShapeDtypeStruct(dims, kind)


def named(table, z, core, block, blocks):
    adapter = table[(z * CORES + core) * blocks + block]
    owner = adapter // 2
    return owner % 2, (owner // 2) * 2 + adapter % 2


def cut(down, up, out):
    parts = out.shape[0] // COPIES
    for k in range(down.shape[0]):
        d, u = down[k].astype(F32), up[k].astype(F32)
        for i in range(parts):
            at = slice(i * GROUP, (i + 1) * GROUP)
            piece = jnp.concatenate([d[at], u[at]], axis=0).astype(BF16)
            for copy in range(COPIES):
                out[copy * parts + i, k] = piece


def means(counts, owned, down, up):
    parts = owned.shape[0] // COPIES
    for k in range(down.shape[0]):
        for i in range(parts):
            piece = owned[i, k].astype(F32)
            for copy in range(1, COPIES):
                piece = piece + owned[copy * parts + i, k].astype(F32)
            piece = piece / counts[k]
            down[k, i * GROUP:(i + 1) * GROUP] = piece[:GROUP]
            up[k, i * GROUP:(i + 1) * GROUP] = piece[GROUP:]


def partner(where, nz, step):
    return lax.rem(where[0] + (1 - 2 * where[1]) * step + nz, nz)


def pick_pieces(nz, table, where, mine, other, *outs):
    core = where[1]
    blocks = outs[0].shape[0]
    for step, out in zip(STEPS, outs):
        z = partner(where, nz, step)
        for b in range(blocks):
            par, row = named(table, z, core, b, blocks)

            @pl.when(par == core)
            def _():
                out[b] = mine[row]

            @pl.when(par != core)
            def _():
                out[b] = other[row]


def sum_parts(got, out):
    total = got[0]
    for i in range(1, got.shape[0]):
        total = total + got[i]
    total = total.astype(BF16)
    for i in range(out.shape[0]):
        out[i] = total


def add_other(keep, other, out):
    out[...] = (keep[...] + other[...].astype(F32)).astype(BF16).reshape(out.shape)


def is_first(dims, axis):
    return lax.broadcasted_iota(jnp.int32, dims, axis) % (2 * GROUP) < GROUP


def rows_of(ref, b):
    return ref[b * BLOCK:(b + 1) * BLOCK, :]


def matrix(pieces, b):
    return jnp.concatenate([p[b] for p in pieces], axis=0)


def partial_sums(acts, cot, *refs):
    pieces, out = refs[:-1], refs[-1]
    lanes = out.shape[1]
    first = is_first((BLOCK, lanes), 1)
    for b in range(pieces[0].shape[0]):
        w = matrix(pieces, b)
        proj, back = dot(rows_of(acts, b), w, NT), dot(rows_of(cot, b), w, NT)
        out[b * BLOCK:(b + 1) * BLOCK, :] = jnp.where(first, proj, SCALE * back)


def swapped(sums, b):
    lanes = sums.shape[1]
    row = lax.broadcasted_iota(jnp.int32, (lanes, lanes), 0)
    col = lax.broadcasted_iota(jnp.int32, (lanes, lanes), 1)
    place = row == jnp.where(is_first((lanes, lanes), 1), col + GROUP, col - GROUP)
    return dot(rows_of(sums, b), place.astype(BF16), NN).astype(BF16)


def block_grads(acts, cot, sums, *outs):
    lanes = sums.shape[1]
    first = is_first((lanes, acts.shape[1]), 0)
    for b in range(outs[0].shape[0]):
        q = swapped(sums, b)
        down, up = dot(q, rows_of(acts, b), TN), dot(q, rows_of(cot, b), TN)
        g = jnp.where(first, down, SCALE * up).astype(BF16)
        for i, out in enumerate(outs):
            out[b] = g[i * 2 * GROUP:(i + 1) * 2 * GROUP]


def outputs(sums, *refs):
    pieces, out, grad = refs[:-2], refs[-2], refs[-1]
    first = is_first((BLOCK, sums.shape[1]), 1)
    for b in range(pieces[0].shape[0]):
        q, w = swapped(sums, b), matrix(pieces, b)
        zero = jnp.zeros_like(q)
        at = slice(b * BLOCK, (b + 1) * BLOCK)
        out[at, :] = (SCALE * dot(jnp.where(first, zero, q), w, NN)).astype(BF16)
        grad[at, :] = dot(jnp.where(first, q, zero), w, NN).astype(BF16)


def sum_pieces(nz, table, where, *refs):
    gots, (keep, send, acc) = refs[:-3], refs[-3:]
    core = where[1]
    half = keep.shape[0]
    blocks = gots[0].shape[0]
    acc[...] = jnp.zeros_like(acc)
    for step, got in zip(STEPS, gots):
        z = partner(where, nz, step)
        for b in range(blocks):
            par, row = named(table, z, core, b, blocks)
            at = par * half + row
            acc[at] = acc[at] + got[b].astype(F32)
    keep[...] = acc[pl.ds(core * half, half)]
    send[...] = acc[pl.ds((1 - core) * half, half)].astype(BF16)


def local(activations, cotangent, adapter_down_weights, adapter_up_weights, table):
    nz, nxy = lax.axis_size("z"), lax.axis_size("xy")
    share, width, rank = adapter_down_weights.shape
    tokens = activations.shape[0]
    blocks = tokens // BLOCK
    piece = (2 * GROUP, width)
    where = jnp.stack([lax.axis_index("z"), lax.axis_index("core")]).astype(jnp.int32)
    swap = [(0, 1), (1, 0)]
    own = nz * share
    slots = (shape((blocks,) + piece, BF16),) * len(STEPS)

    def over_z(x):
        return lax.all_to_all(x, "z", 0, 0, tiled=True)

    def shift(x, step):
        if step == 0:
            return x
        pairs = [(z * CORES + c, (z + (step, -step)[c]) % nz * CORES + c) for z in range(nz) for c in range(CORES)]
        return lax.ppermute(x, ("z", "core"), pairs)

    def total(part):
        rows = part.shape[0] // nxy
        got = lax.all_to_all(part.reshape(nxy, rows, part.shape[1]), "xy", 0, 0, tiled=True)
        spread = call(sum_parts, shape(got.shape, BF16), (got,), [VMEM])
        return lax.all_to_all(spread, "xy", 0, 0, tiled=True).reshape(part.shape)

    down = jnp.swapaxes(adapter_down_weights, 1, 2)
    spread = call(cut, shape((nz, share) + piece, BF16), (down, adapter_up_weights), [VMEM] * 2)
    held = over_z(spread).reshape(own, *piece)
    held_other = lax.ppermute(held, "core", swap)
    wanted = call(
        functools.partial(pick_pieces, nz), slots, (table, where, held, held_other), [SMEM, SMEM, VMEM, VMEM]
    )
    pieces = [shift(w, step) for w, step in zip(wanted, STEPS)]
    ids = (where[0] * CORES + where[1]) * share + jnp.arange(share, dtype=jnp.int32)
    counts = jnp.sum((table[:, None] == ids[None, :]).astype(F32), axis=0) * BLOCK
    pieces, counts = lax.optimization_barrier((pieces, counts))
    sums = total(
        call(
            partial_sums, shape((tokens, 2 * rank), F32), (activations, cotangent, *pieces), [VMEM] * (2 + len(STEPS))
        )
    )
    parts = call(block_grads, slots, (activations, cotangent, sums), [VMEM] * 3)
    gots = [shift(g, -step) for g, step in zip(parts, STEPS)]
    out, grad = call(outputs, (shape((tokens, width), BF16),) * 2, (sums, *pieces), [VMEM] * (1 + len(STEPS)))
    gots, out, grad = lax.optimization_barrier((gots, out, grad))
    keep, send = call(
        functools.partial(sum_pieces, nz), (shape((own,) + piece, F32), shape((own,) + piece, BF16)),
        (table, where, *gots), [SMEM, SMEM] + [VMEM] * len(STEPS), [pltpu.VMEM((CORES * own,) + piece, F32)],
    )
    from_other = lax.ppermute(send, "core", swap)
    merged = call(add_other, shape((nz, share) + piece, BF16), (keep, from_other), [VMEM] * 2)
    owned = over_z(merged)
    down_grad, up_grad = call(means, (shape((share, rank, width), F32),) * 2, (counts, owned), [SMEM, VMEM])
    return out, grad, jnp.swapaxes(down_grad, 1, 2), up_grad


def solution(mesh):
    nxy = mesh.shape["adapter"]
    grid = Mesh(mesh.devices.reshape(-1, CORES, nxy), ("z", "core", "xy"))
    dp = ("z", "core")
    specs = (P(dp, "xy"), P(dp, "xy"), P(dp, "xy", None), P(dp, None, "xy"))
    return jax.shard_map(
        local, mesh=grid, in_specs=specs + (P(),), out_specs=specs, check_vma=False
    )
```

```python
import functools

import jax
import jax.numpy as jnp
from jax import lax
from jax.experimental import pallas as pl
from jax.experimental.pallas import tpu as pltpu
from jax.sharding import Mesh, PartitionSpec as P

BLOCK = 128
SCALE = 2.0
CORES = 2
COPIES = 2
GROUP = 8
STEPS = (0, 4, -3, 3, -2, 2, -1, 1)
HALVES = (slice(0, 4), slice(4, 8))
F32, BF16 = jnp.float32, jnp.bfloat16

VMEM = pl.BlockSpec(memory_space=pltpu.VMEM)
SMEM = pl.BlockSpec(memory_space=pltpu.SMEM)
NT = (((1,), (1,)), ((), ()))
NN = (((1,), (0,)), ((), ()))
TN = (((0,), (0,)), ((), ()))


def dot(a, b, dims):
    return lax.dot_general(a, b, dims, preferred_element_type=F32)


def call(body, outs, ins, in_specs, scratch=()):
    return pl.pallas_call(
        body,
        out_shape=outs,
        in_specs=in_specs,
        out_specs=jax.tree.map(lambda _: VMEM, outs),
        scratch_shapes=list(scratch),
        compiler_params=pltpu.CompilerParams(vmem_limit_bytes=40 * 2**20),
    )(*ins)


def shape(dims, kind):
    return jax.ShapeDtypeStruct(dims, kind)


def named(table, z, core, block, blocks):
    adapter = table[(z * CORES + core) * blocks + block]
    owner = adapter // 2
    return owner % 2, (owner // 2) * 2 + adapter % 2


def cut(down, up, out):
    parts = out.shape[0] // COPIES
    for k in range(down.shape[0]):
        d, u = down[k].astype(F32), up[k].astype(F32)
        for i in range(parts):
            at = slice(i * GROUP, (i + 1) * GROUP)
            piece = jnp.concatenate([d[at], u[at]], axis=0).astype(BF16)
            for copy in range(COPIES):
                out[copy * parts + i, k] = piece


def means(counts, owned, down, up):
    parts = owned.shape[0] // COPIES
    for k in range(down.shape[0]):
        for i in range(parts):
            piece = owned[i, k].astype(F32)
            for copy in range(1, COPIES):
                piece = piece + owned[copy * parts + i, k].astype(F32)
            piece = piece / counts[k]
            down[k, i * GROUP:(i + 1) * GROUP] = piece[:GROUP]
            up[k, i * GROUP:(i + 1) * GROUP] = piece[GROUP:]


def partner(where, nz, step):
    return lax.rem(where[0] + (1 - 2 * where[1]) * step + nz, nz)


def pick_pieces(nz, table, where, mine, other, *outs):
    core = where[1]
    blocks = outs[0].shape[0]
    for step, out in zip(STEPS, outs):
        z = partner(where, nz, step)
        for b in range(blocks):
            par, row = named(table, z, core, b, blocks)

            @pl.when(par == core)
            def _():
                out[b] = mine[row]

            @pl.when(par != core)
            def _():
                out[b] = other[row]


def sum_parts(got, out):
    total = got[0]
    for i in range(1, got.shape[0]):
        total = total + got[i]
    total = total.astype(BF16)
    for i in range(out.shape[0]):
        out[i] = total


def add_other(keep, other, out):
    out[...] = (keep[...] + other[...].astype(F32)).astype(BF16).reshape(out.shape)


def is_first(dims, axis):
    return lax.broadcasted_iota(jnp.int32, dims, axis) % (2 * GROUP) < GROUP


def rows_of(ref, b):
    return ref[b * BLOCK:(b + 1) * BLOCK, :]


def matrix(pieces, b, blocks):
    w = jnp.concatenate([p[b] for p in pieces], axis=0)
    zero = jnp.zeros_like(w)
    return jnp.concatenate([w, zero] if b < blocks // 2 else [zero, w], axis=0)


def partial_sums(acts, cot, *refs):
    pieces, out = refs[:-1], refs[-1]
    blocks = pieces[0].shape[0]
    first = is_first((BLOCK, out.shape[1]), 1)
    for j in range(blocks // 2):
        proj, back = 0, 0
        for b in (j, j + blocks // 2):
            w = matrix(pieces, b, blocks)
            proj, back = proj + dot(rows_of(acts, b), w, NT), back + dot(rows_of(cot, b), w, NT)
        out[j * BLOCK:(j + 1) * BLOCK, :] = jnp.where(first, proj, SCALE * back)


def swapped(sums, b):
    lanes = sums.shape[1]
    row = lax.broadcasted_iota(jnp.int32, (lanes, lanes), 0)
    col = lax.broadcasted_iota(jnp.int32, (lanes, lanes), 1)
    place = row == jnp.where(is_first((lanes, lanes), 1), col + GROUP, col - GROUP)
    return dot(rows_of(sums, b), place.astype(BF16), NN).astype(BF16)


def block_grads(acts, cot, sums, *outs):
    blocks = outs[0].shape[0]
    lanes = sums.shape[1]
    first = is_first((lanes, acts.shape[1]), 0)
    for j in range(blocks // 2):
        q = swapped(sums, j)
        for at, b in ((0, j), (lanes // 2, j + blocks // 2)):
            down, up = dot(q, rows_of(acts, b), TN), dot(q, rows_of(cot, b), TN)
            g = jnp.where(first, down, SCALE * up).astype(BF16)
            for i, out in enumerate(outs):
                out[b] = g[at + i * 2 * GROUP:at + (i + 1) * 2 * GROUP]


def outputs(sums_a, sums_b, *refs):
    pieces, out, grad = refs[:-2], refs[-2], refs[-1]
    blocks = pieces[0].shape[0]
    first = is_first((BLOCK, sums_a.shape[1]), 1)
    zero = jnp.zeros((BLOCK, sums_a.shape[1]), BF16)
    for j in range(blocks // 2):
        qs = [swapped(sums, j) for sums in (sums_a, sums_b)]
        for b in (j, j + blocks // 2):
            up, down = 0, 0
            for q, half in zip(qs, HALVES):
                w = matrix(pieces[half], b, blocks)
                up = up + dot(jnp.where(first, zero, q), w, NN)
                down = down + dot(jnp.where(first, q, zero), w, NN)
            at = slice(b * BLOCK, (b + 1) * BLOCK)
            out[at, :] = (SCALE * up).astype(BF16)
            grad[at, :] = down.astype(BF16)


def sum_pieces(nz, table, where, *refs):
    gots, (keep, send, acc) = refs[:-3], refs[-3:]
    core = where[1]
    half = keep.shape[0]
    blocks = gots[0].shape[0]
    acc[...] = jnp.zeros_like(acc)
    for step, got in zip(STEPS, gots):
        z = partner(where, nz, step)
        for b in range(blocks):
            par, row = named(table, z, core, b, blocks)
            at = par * half + row
            acc[at] = acc[at] + got[b].astype(F32)
    keep[...] = acc[pl.ds(core * half, half)]
    send[...] = acc[pl.ds((1 - core) * half, half)].astype(BF16)


def local(activations, cotangent, adapter_down_weights, adapter_up_weights, table):
    nz, nxy = lax.axis_size("z"), lax.axis_size("xy")
    share, width, rank = adapter_down_weights.shape
    tokens = activations.shape[0]
    blocks = tokens // BLOCK
    piece = (2 * GROUP, width)
    where = jnp.stack([lax.axis_index("z"), lax.axis_index("core")]).astype(jnp.int32)
    swap = [(0, 1), (1, 0)]
    own = nz * share
    slots = (shape((blocks,) + piece, BF16),) * len(STEPS)

    def over_z(x):
        return lax.all_to_all(x, "z", 0, 0, tiled=True)

    def shift(x, step):
        if step == 0:
            return x
        pairs = [(z * CORES + c, (z + (step, -step)[c]) % nz * CORES + c) for z in range(nz) for c in range(CORES)]
        return lax.ppermute(x, ("z", "core"), pairs)

    def total(part):
        rows = part.shape[0] // nxy
        got = lax.all_to_all(part.reshape(nxy, rows, part.shape[1]), "xy", 0, 0, tiled=True)
        spread = call(sum_parts, shape(got.shape, BF16), (got,), [VMEM])
        return lax.all_to_all(spread, "xy", 0, 0, tiled=True).reshape(part.shape)

    down = jnp.swapaxes(adapter_down_weights, 1, 2)
    spread = call(cut, shape((nz, share) + piece, BF16), (down, adapter_up_weights), [VMEM] * 2)
    held = over_z(spread).reshape(own, *piece)
    held_other = lax.ppermute(held, "core", swap)
    wanted = call(
        functools.partial(pick_pieces, nz), slots, (table, where, held, held_other), [SMEM, SMEM, VMEM, VMEM]
    )
    pieces = [shift(w, step) for w, step in zip(wanted, STEPS)]
    ids = (where[0] * CORES + where[1]) * share + jnp.arange(share, dtype=jnp.int32)
    counts = jnp.sum((table[:, None] == ids[None, :]).astype(F32), axis=0) * BLOCK
    pieces[-1], counts = lax.optimization_barrier((pieces[-1], counts))
    sums, gots = [], []
    for half in HALVES:
        some, steps = pieces[half], STEPS[half]
        part = call(
            partial_sums, shape((tokens // 2, 2 * rank), F32), (activations, cotangent, *some), [VMEM] * (2 + len(some))
        )
        sums.append(total(part))
        parts = call(block_grads, slots[half], (activations, cotangent, sums[-1]), [VMEM] * 3)
        gots += [shift(g, -step) for g, step in zip(parts, steps)]
    out, grad = call(outputs, (shape((tokens, width), BF16),) * 2, (*sums, *pieces), [VMEM] * (2 + len(STEPS)))
    gots, out, grad = lax.optimization_barrier((gots, out, grad))
    keep, send = call(
        functools.partial(sum_pieces, nz), (shape((own,) + piece, F32), shape((own,) + piece, BF16)),
        (table, where, *gots), [SMEM, SMEM] + [VMEM] * len(STEPS), [pltpu.VMEM((CORES * own,) + piece, F32)],
    )
    from_other = lax.ppermute(send, "core", swap)
    merged = call(add_other, shape((nz, share) + piece, BF16), (keep, from_other), [VMEM] * 2)
    owned = over_z(merged)
    down_grad, up_grad = call(means, (shape((share, rank, width), F32),) * 2, (counts, owned), [SMEM, VMEM])
    return out, grad, jnp.swapaxes(down_grad, 1, 2), up_grad


def solution(mesh):
    nxy = mesh.shape["adapter"]
    grid = Mesh(mesh.devices.reshape(-1, CORES, nxy), ("z", "core", "xy"))
    dp = ("z", "core")
    specs = (P(dp, "xy"), P(dp, "xy"), P(dp, "xy", None), P(dp, None, "xy"))
    return jax.shard_map(
        local, mesh=grid, in_specs=specs + (P(),), out_specs=specs, check_vma=False
    )
```

```python
import functools

import jax
import jax.numpy as jnp
from jax import lax
from jax.experimental import pallas as pl
from jax.experimental.pallas import tpu as pltpu
from jax.sharding import Mesh, PartitionSpec as P

BLOCK = 128
SCALE = 2.0
CORES = 2
COPIES = 2
GROUP = 8
STEPS = (0, 4, -3, 3, -2, 2, -1, 1)
F32, BF16 = jnp.float32, jnp.bfloat16

VMEM = pl.BlockSpec(memory_space=pltpu.VMEM)
SMEM = pl.BlockSpec(memory_space=pltpu.SMEM)
HBM = pl.BlockSpec(memory_space=pltpu.HBM)
NT = (((1,), (1,)), ((), ()))
NN = (((1,), (0,)), ((), ()))
TN = (((0,), (0,)), ((), ()))


def dot(a, b, dims):
    return lax.dot_general(a, b, dims, preferred_element_type=F32)


def call(body, outs, ins, in_specs, scratch=()):
    return pl.pallas_call(
        body,
        out_shape=outs,
        in_specs=in_specs,
        out_specs=jax.tree.map(lambda _: VMEM, outs),
        scratch_shapes=list(scratch),
        compiler_params=pltpu.CompilerParams(vmem_limit_bytes=40 * 2**20),
    )(*ins)


def shape(dims, kind):
    return jax.ShapeDtypeStruct(dims, kind)


def named(table, z, core, block, blocks):
    adapter = table[(z * CORES + core) * blocks + block]
    owner = adapter // 2
    return owner % 2, (owner // 2) * 2 + adapter % 2


def cut(down_hbm, up_hbm, out, down, up, sems):
    copies = [pltpu.make_async_copy(down_hbm, down, sems.at[0]), pltpu.make_async_copy(up_hbm, up, sems.at[1])]
    for copy in copies:
        copy.start()
    for copy in copies:
        copy.wait()
    parts = out.shape[0] // COPIES
    for k in range(down.shape[0]):
        d, u = down[k].astype(F32), up[k].astype(F32)
        for i in range(parts):
            at = slice(i * GROUP, (i + 1) * GROUP)
            piece = jnp.concatenate([d[at], u[at]], axis=0).astype(BF16)
            for copy in range(COPIES):
                out[copy * parts + i, k] = piece


def means(counts, owned, down, up):
    parts = owned.shape[0] // COPIES
    for k in range(down.shape[0]):
        for i in range(parts):
            piece = owned[i, k].astype(F32)
            for copy in range(1, COPIES):
                piece = piece + owned[copy * parts + i, k].astype(F32)
            piece = piece / counts[k]
            down[k, i * GROUP:(i + 1) * GROUP] = piece[:GROUP]
            up[k, i * GROUP:(i + 1) * GROUP] = piece[GROUP:]


def partner(where, nz, step):
    return lax.rem(where[0] + (1 - 2 * where[1]) * step + nz, nz)


def pick_pieces(nz, table, where, mine, other, *outs):
    core = where[1]
    blocks = outs[0].shape[0]
    for step, out in zip(STEPS, outs):
        z = partner(where, nz, step)
        for b in range(blocks):
            par, row = named(table, z, core, b, blocks)

            @pl.when(par == core)
            def _():
                out[b] = mine[row]

            @pl.when(par != core)
            def _():
                out[b] = other[row]


def sum_parts(got, out):
    total = got[0]
    for i in range(1, got.shape[0]):
        total = total + got[i]
    total = total.astype(BF16)
    for i in range(out.shape[0]):
        out[i] = total


def add_other(keep, other, out):
    out[...] = (keep[...] + other[...].astype(F32)).astype(BF16).reshape(out.shape)


def is_first(dims, axis):
    return lax.broadcasted_iota(jnp.int32, dims, axis) % (2 * GROUP) < GROUP


def rows_of(ref, b):
    return ref[b * BLOCK:(b + 1) * BLOCK, :]


def matrix(pieces, b):
    return jnp.concatenate([p[b] for p in pieces], axis=0)


def partial_sums(acts, cot, *refs):
    pieces, out = refs[:-1], refs[-1]
    lanes = out.shape[1]
    first = is_first((BLOCK, lanes), 1)
    for b in range(pieces[0].shape[0]):
        w = matrix(pieces, b)
        proj, back = dot(rows_of(acts, b), w, NT), dot(rows_of(cot, b), w, NT)
        out[b * BLOCK:(b + 1) * BLOCK, :] = jnp.where(first, proj, SCALE * back)


def swap_matrix(lanes):
    row = lax.broadcasted_iota(jnp.int32, (lanes, lanes), 0)
    col = lax.broadcasted_iota(jnp.int32, (lanes, lanes), 1)
    return (row == jnp.where(is_first((lanes, lanes), 1), col + GROUP, col - GROUP)).astype(BF16)


def block_grads(acts, cot, sums, *outs):
    lanes = sums.shape[1]
    first = is_first((lanes, acts.shape[1]), 0)
    place = swap_matrix(lanes)
    for b in range(outs[0].shape[0]):
        q = dot(place, rows_of(sums, b), NT).astype(BF16)
        down, up = dot(q, rows_of(acts, b), NN), dot(q, rows_of(cot, b), NN)
        g = jnp.where(first, down, SCALE * up).astype(BF16)
        for i, out in enumerate(outs):
            out[b] = g[i * 2 * GROUP:(i + 1) * 2 * GROUP]


def outputs(sums, *refs):
    pieces, out, grad = refs[:-2], refs[-2], refs[-1]
    first = is_first((BLOCK, sums.shape[1]), 1)
    place = swap_matrix(sums.shape[1])
    for b in range(pieces[0].shape[0]):
        q, w = dot(rows_of(sums, b), place, NN).astype(BF16), matrix(pieces, b)
        zero = jnp.zeros_like(q)
        at = slice(b * BLOCK, (b + 1) * BLOCK)
        out[at, :] = (SCALE * dot(jnp.where(first, zero, q), w, NN)).astype(BF16)
        grad[at, :] = dot(jnp.where(first, q, zero), w, NN).astype(BF16)


def sum_pieces(nz, table, where, *refs):
    gots, (keep, send, acc) = refs[:-3], refs[-3:]
    core = where[1]
    half = keep.shape[0]
    blocks = gots[0].shape[0]
    acc[...] = jnp.zeros_like(acc)
    for step, got in zip(STEPS, gots):
        z = partner(where, nz, step)
        for b in range(blocks):
            par, row = named(table, z, core, b, blocks)
            at = par * half + row
            acc[at] = acc[at] + got[b].astype(F32)
    keep[...] = acc[pl.ds(core * half, half)]
    send[...] = acc[pl.ds((1 - core) * half, half)].astype(BF16)


def local(activations, cotangent, adapter_down_weights, adapter_up_weights, table):
    nz, nxy = lax.axis_size("z"), lax.axis_size("xy")
    share, width, rank = adapter_down_weights.shape
    tokens = activations.shape[0]
    blocks = tokens // BLOCK
    piece = (2 * GROUP, width)
    where = jnp.stack([lax.axis_index("z"), lax.axis_index("core")]).astype(jnp.int32)
    swap = [(0, 1), (1, 0)]
    own = nz * share
    slots = (shape((blocks,) + piece, BF16),) * len(STEPS)

    def over_z(x):
        return lax.all_to_all(x, "z", 0, 0, tiled=True)

    def shift(x, step):
        if step == 0:
            return x
        pairs = [(z * CORES + c, (z + (step, -step)[c]) % nz * CORES + c) for z in range(nz) for c in range(CORES)]
        return lax.ppermute(x, ("z", "core"), pairs)

    def total(part):
        rows = part.shape[0] // nxy
        got = lax.all_to_all(part.reshape(nxy, rows, part.shape[1]), "xy", 0, 0, tiled=True)
        spread = call(sum_parts, shape(got.shape, BF16), (got,), [VMEM])
        return lax.all_to_all(spread, "xy", 0, 0, tiled=True).reshape(part.shape)

    down = jnp.swapaxes(adapter_down_weights, 1, 2)
    both = [pltpu.VMEM(down.shape, BF16)] * 2 + [pltpu.SemaphoreType.DMA((2,))]
    spread = call(cut, shape((nz, share) + piece, BF16), (down, adapter_up_weights), [HBM] * 2, both)
    held = over_z(spread).reshape(own, *piece)
    held_other = lax.ppermute(held, "core", swap)
    wanted = call(
        functools.partial(pick_pieces, nz), slots, (table, where, held, held_other), [SMEM, SMEM, VMEM, VMEM]
    )
    pieces = [shift(w, step) for w, step in zip(wanted, STEPS)]
    ids = (where[0] * CORES + where[1]) * share + jnp.arange(share, dtype=jnp.int32)
    counts = jnp.sum((table[:, None] == ids[None, :]).astype(F32), axis=0) * BLOCK
    pieces, counts = lax.optimization_barrier((pieces, counts))
    sums = total(
        call(
            partial_sums, shape((tokens, 2 * rank), F32), (activations, cotangent, *pieces), [VMEM] * (2 + len(STEPS))
        )
    )
    parts = call(block_grads, slots, (activations, cotangent, sums), [VMEM] * 3)
    gots = [shift(g, -step) for g, step in zip(parts, STEPS)]
    out, grad = call(outputs, (shape((tokens, width), BF16),) * 2, (sums, *pieces), [VMEM] * (1 + len(STEPS)))
    gots, out, grad = lax.optimization_barrier((gots, out, grad))
    keep, send = call(
        functools.partial(sum_pieces, nz), (shape((own,) + piece, F32), shape((own,) + piece, BF16)),
        (table, where, *gots), [SMEM, SMEM] + [VMEM] * len(STEPS), [pltpu.VMEM((CORES * own,) + piece, F32)],
    )
    from_other = lax.ppermute(send, "core", swap)
    merged = call(add_other, shape((nz, share) + piece, BF16), (keep, from_other), [VMEM] * 2)
    owned = over_z(merged)
    down_grad, up_grad = call(means, (shape((share, rank, width), F32),) * 2, (counts, owned), [SMEM, VMEM])
    return out, grad, jnp.swapaxes(down_grad, 1, 2), up_grad


def solution(mesh):
    nxy = mesh.shape["adapter"]
    grid = Mesh(mesh.devices.reshape(-1, CORES, nxy), ("z", "core", "xy"))
    dp = ("z", "core")
    specs = (P(dp, "xy"), P(dp, "xy"), P(dp, "xy", None), P(dp, None, "xy"))
    return jax.shard_map(
        local, mesh=grid, in_specs=specs + (P(),), out_specs=specs, check_vma=False
    )
```

```python
import functools

import jax
import jax.numpy as jnp
from jax import lax
from jax.experimental import pallas as pl
from jax.experimental.pallas import tpu as pltpu
from jax.sharding import Mesh, PartitionSpec as P

BLOCK = 128
SCALE = 2.0
CORES = 2
COPIES = 2
GROUP = 8
STEPS = (0, 4, -3, 3, -2, 2, -1, 1)
F32, BF16 = jnp.float32, jnp.bfloat16

VMEM = pl.BlockSpec(memory_space=pltpu.VMEM)
SMEM = pl.BlockSpec(memory_space=pltpu.SMEM)
HBM = pl.BlockSpec(memory_space=pltpu.HBM)
NT = (((1,), (1,)), ((), ()))
NN = (((1,), (0,)), ((), ()))
TN = (((0,), (0,)), ((), ()))


def dot(a, b, dims):
    return lax.dot_general(a, b, dims, preferred_element_type=F32)


def call(body, outs, ins, in_specs, scratch=(), room=40):
    return pl.pallas_call(
        body,
        out_shape=outs,
        in_specs=in_specs,
        out_specs=jax.tree.map(lambda _: VMEM, outs),
        scratch_shapes=list(scratch),
        compiler_params=pltpu.CompilerParams(vmem_limit_bytes=room * 2**20),
    )(*ins)


def shape(dims, kind):
    return jax.ShapeDtypeStruct(dims, kind)


def named(table, z, core, block, blocks):
    adapter = table[(z * CORES + core) * blocks + block]
    owner = adapter // 2
    return owner % 2, (owner // 2) * 2 + adapter % 2


def cut(down_hbm, up_hbm, out, down, up, sems):
    copies = [pltpu.make_async_copy(down_hbm, down, sems.at[0]), pltpu.make_async_copy(up_hbm, up, sems.at[1])]
    for copy in copies:
        copy.start()
    for copy in copies:
        copy.wait()
    parts = out.shape[0] // COPIES
    for k in range(down.shape[0]):
        d, u = down[k].astype(F32), up[k].astype(F32)
        for i in range(parts):
            at = slice(i * GROUP, (i + 1) * GROUP)
            piece = jnp.concatenate([d[at], u[at]], axis=0).astype(BF16)
            for copy in range(COPIES):
                out[copy * parts + i, k] = piece


def means(counts, owned, down, up):
    parts = owned.shape[0] // COPIES
    for k in range(down.shape[0]):
        for i in range(parts):
            piece = owned[i, k].astype(F32)
            for copy in range(1, COPIES):
                piece = piece + owned[copy * parts + i, k].astype(F32)
            piece = piece / counts[k]
            down[k, i * GROUP:(i + 1) * GROUP] = piece[:GROUP]
            up[k, i * GROUP:(i + 1) * GROUP] = piece[GROUP:]


def partner(where, nz, step):
    return lax.rem(where[0] + (1 - 2 * where[1]) * step + nz, nz)


def pick_pieces(nz, table, where, mine, other, *outs):
    core = where[1]
    blocks = outs[0].shape[0]
    for step, out in zip(STEPS, outs):
        z = partner(where, nz, step)
        for b in range(blocks):
            par, row = named(table, z, core, b, blocks)

            @pl.when(par == core)
            def _():
                out[b] = mine[row]

            @pl.when(par != core)
            def _():
                out[b] = other[row]


def sum_parts(got, out):
    total = got[0]
    for i in range(1, got.shape[0]):
        total = total + got[i]
    total = total.astype(BF16)
    for i in range(out.shape[0]):
        out[i] = total


def add_other(keep, other, out):
    out[...] = (keep[...] + other[...].astype(F32)).astype(BF16).reshape(out.shape)


def is_first(dims, axis):
    return lax.broadcasted_iota(jnp.int32, dims, axis) % (2 * GROUP) < GROUP


def rows_of(ref, b):
    return ref[b * BLOCK:(b + 1) * BLOCK, :]


def matrix(pieces, b):
    return jnp.concatenate([p[b] for p in pieces], axis=0)


def partial_sums(acts, cot, *refs):
    pieces, out = refs[:-1], refs[-1]
    lanes = out.shape[1]
    first = is_first((BLOCK, lanes), 1)
    for b in range(pieces[0].shape[0]):
        w = matrix(pieces, b)
        proj, back = dot(rows_of(acts, b), w, NT), dot(rows_of(cot, b), w, NT)
        out[b * BLOCK:(b + 1) * BLOCK, :] = jnp.where(first, proj, SCALE * back)


def swap_matrix(lanes):
    row = lax.broadcasted_iota(jnp.int32, (lanes, lanes), 0)
    col = lax.broadcasted_iota(jnp.int32, (lanes, lanes), 1)
    return (row == jnp.where(is_first((lanes, lanes), 1), col + GROUP, col - GROUP)).astype(BF16)


def block_grads(acts, cot, sums, *outs):
    lanes = sums.shape[1]
    first = is_first((lanes, acts.shape[1]), 0)
    place = swap_matrix(lanes)
    for b in range(outs[0].shape[0]):
        q = dot(place, rows_of(sums, b), NT).astype(BF16)
        down, up = dot(q, rows_of(acts, b), NN), dot(q, rows_of(cot, b), NN)
        g = jnp.where(first, down, SCALE * up).astype(BF16)
        for i, out in enumerate(outs):
            out[b] = g[i * 2 * GROUP:(i + 1) * 2 * GROUP]


def outputs(sums, *refs):
    pieces, out, grad = refs[:-2], refs[-2], refs[-1]
    first = is_first((BLOCK, sums.shape[1]), 1)
    place = swap_matrix(sums.shape[1])
    for b in range(pieces[0].shape[0]):
        q, w = dot(rows_of(sums, b), place, NN).astype(BF16), matrix(pieces, b)
        zero = jnp.zeros_like(q)
        at = slice(b * BLOCK, (b + 1) * BLOCK)
        out[at, :] = (SCALE * dot(jnp.where(first, zero, q), w, NN)).astype(BF16)
        grad[at, :] = dot(jnp.where(first, q, zero), w, NN).astype(BF16)


def sum_pieces(nz, kept, table, where, *refs):
    gots, (out, acc) = refs[:-2], refs[-2:]
    core = where[1] if kept else 1 - where[1]
    blocks = gots[0].shape[0]
    acc[...] = jnp.zeros_like(acc)
    for step, got in zip(STEPS, gots):
        z = partner(where, nz, step)
        for b in range(blocks):
            par, row = named(table, z, where[1], b, blocks)

            @pl.when(par == core)
            def _():
                acc[row] = acc[row] + got[b].astype(F32)

    out[...] = acc[...].astype(out.dtype)


def local(activations, cotangent, adapter_down_weights, adapter_up_weights, table):
    nz, nxy = lax.axis_size("z"), lax.axis_size("xy")
    share, width, rank = adapter_down_weights.shape
    tokens = activations.shape[0]
    blocks = tokens // BLOCK
    piece = (2 * GROUP, width)
    where = jnp.stack([lax.axis_index("z"), lax.axis_index("core")]).astype(jnp.int32)
    swap = [(0, 1), (1, 0)]
    own = nz * share
    slots = (shape((blocks,) + piece, BF16),) * len(STEPS)

    def over_z(x):
        return lax.all_to_all(x, "z", 0, 0, tiled=True)

    def shift(x, step):
        if step == 0:
            return x
        pairs = [(z * CORES + c, (z + (step, -step)[c]) % nz * CORES + c) for z in range(nz) for c in range(CORES)]
        return lax.ppermute(x, ("z", "core"), pairs)

    def total(part):
        rows = part.shape[0] // nxy
        got = lax.all_to_all(part.reshape(nxy, rows, part.shape[1]), "xy", 0, 0, tiled=True)
        spread = call(sum_parts, shape(got.shape, BF16), (got,), [VMEM])
        return lax.all_to_all(spread, "xy", 0, 0, tiled=True).reshape(part.shape)

    down = jnp.swapaxes(adapter_down_weights, 1, 2)
    both = [pltpu.VMEM(down.shape, BF16)] * 2 + [pltpu.SemaphoreType.DMA((2,))]
    spread = call(cut, shape((nz, share) + piece, BF16), (down, adapter_up_weights), [HBM] * 2, both, 60)
    held = over_z(spread).reshape(own, *piece)
    held_other = lax.ppermute(held, "core", swap)
    wanted = call(
        functools.partial(pick_pieces, nz), slots, (table, where, held, held_other), [SMEM, SMEM, VMEM, VMEM]
    )
    pieces = [shift(w, step) for w, step in zip(wanted, STEPS)]
    ids = (where[0] * CORES + where[1]) * share + jnp.arange(share, dtype=jnp.int32)
    counts = jnp.sum((table[:, None] == ids[None, :]).astype(F32), axis=0) * BLOCK
    pieces, counts = lax.optimization_barrier((pieces, counts))
    sums = total(
        call(
            partial_sums, shape((tokens, 2 * rank), F32), (activations, cotangent, *pieces), [VMEM] * (2 + len(STEPS))
        )
    )
    parts = call(block_grads, slots, (activations, cotangent, sums), [VMEM] * 3)
    gots = [shift(g, -step) for g, step in zip(parts, STEPS)]
    def summed(kept, kind):
        return call(
            functools.partial(sum_pieces, nz, kept), shape((own,) + piece, kind), (table, where, *gots),
            [SMEM, SMEM] + [VMEM] * len(STEPS), [pltpu.VMEM((own,) + piece, F32)],
        )

    from_other = lax.ppermute(summed(False, BF16), "core", swap)
    merged = call(add_other, shape((nz, share) + piece, BF16), (summed(True, F32), from_other), [VMEM] * 2)
    owned = over_z(merged)
    out, grad = call(outputs, (shape((tokens, width), BF16),) * 2, (sums, *pieces), [VMEM] * (1 + len(STEPS)))
    down_grad, up_grad = call(means, (shape((share, rank, width), F32),) * 2, (counts, owned), [SMEM, VMEM])
    return out, grad, jnp.swapaxes(down_grad, 1, 2), up_grad


def solution(mesh):
    nxy = mesh.shape["adapter"]
    grid = Mesh(mesh.devices.reshape(-1, CORES, nxy), ("z", "core", "xy"))
    dp = ("z", "core")
    specs = (P(dp, "xy"), P(dp, "xy"), P(dp, "xy", None), P(dp, None, "xy"))
    return jax.shard_map(
        local, mesh=grid, in_specs=specs + (P(),), out_specs=specs, check_vma=False
    )
```

```python
import functools

import jax
import jax.numpy as jnp
from jax import lax
from jax.experimental import pallas as pl
from jax.experimental.pallas import tpu as pltpu
from jax.sharding import Mesh, PartitionSpec as P

BLOCK = 128
SCALE = 2.0
CORES = 2
COPIES = 2
GROUP = 8
STEPS = (4, -3, 3, -2, 2, -1, 1, 0)
FIRST, REST = slice(0, 2), slice(2, 8)
F32, BF16 = jnp.float32, jnp.bfloat16

VMEM = pl.BlockSpec(memory_space=pltpu.VMEM)
SMEM = pl.BlockSpec(memory_space=pltpu.SMEM)
HBM = pl.BlockSpec(memory_space=pltpu.HBM)
NT = (((1,), (1,)), ((), ()))
NN = (((1,), (0,)), ((), ()))
TN = (((0,), (0,)), ((), ()))


def dot(a, b, dims):
    return lax.dot_general(a, b, dims, preferred_element_type=F32)


def call(body, outs, ins, in_specs, scratch=()):
    return pl.pallas_call(
        body,
        out_shape=outs,
        in_specs=in_specs,
        out_specs=jax.tree.map(lambda _: VMEM, outs),
        scratch_shapes=list(scratch),
        compiler_params=pltpu.CompilerParams(vmem_limit_bytes=40 * 2**20),
    )(*ins)


def shape(dims, kind):
    return jax.ShapeDtypeStruct(dims, kind)


def named(table, z, core, block, blocks):
    adapter = table[(z * CORES + core) * blocks + block]
    owner = adapter // 2
    return owner % 2, (owner // 2) * 2 + adapter % 2


def cut(down_hbm, up_hbm, out, down, up, sems):
    copies = [pltpu.make_async_copy(down_hbm, down, sems.at[0]), pltpu.make_async_copy(up_hbm, up, sems.at[1])]
    for copy in copies:
        copy.start()
    for copy in copies:
        copy.wait()
    parts = out.shape[0] // COPIES
    for k in range(down.shape[0]):
        d, u = down[k].astype(F32), up[k].astype(F32)
        for i in range(parts):
            at = slice(i * GROUP, (i + 1) * GROUP)
            piece = jnp.concatenate([d[at], u[at]], axis=0).astype(BF16)
            for copy in range(COPIES):
                out[copy * parts + i, k] = piece


def means(counts, owned, down, up):
    parts = owned.shape[0] // COPIES
    for k in range(down.shape[0]):
        for i in range(parts):
            piece = owned[i, k].astype(F32)
            for copy in range(1, COPIES):
                piece = piece + owned[copy * parts + i, k].astype(F32)
            piece = piece / counts[k]
            down[k, i * GROUP:(i + 1) * GROUP] = piece[:GROUP]
            up[k, i * GROUP:(i + 1) * GROUP] = piece[GROUP:]


def partner(where, nz, step):
    return lax.rem(where[0] + (1 - 2 * where[1]) * step + nz, nz)


def pick_pieces(nz, steps, table, where, mine, other, *outs):
    core = where[1]
    blocks = outs[0].shape[0]
    for step, out in zip(steps, outs):
        z = partner(where, nz, step)
        for b in range(blocks):
            par, row = named(table, z, core, b, blocks)

            @pl.when(par == core)
            def _():
                out[b] = mine[row]

            @pl.when(par != core)
            def _():
                out[b] = other[row]


def sum_parts(got, out):
    total = got[0]
    for i in range(1, got.shape[0]):
        total = total + got[i]
    total = total.astype(BF16)
    for i in range(out.shape[0]):
        out[i] = total


def add_other(keep, other, out):
    out[...] = (keep[...] + other[...].astype(F32)).astype(BF16).reshape(out.shape)


def is_first(dims, axis):
    return lax.broadcasted_iota(jnp.int32, dims, axis) % (2 * GROUP) < GROUP


def rows_of(ref, b):
    return ref[b * BLOCK:(b + 1) * BLOCK, :]


def matrix(pieces, b):
    return jnp.concatenate([p[b] for p in pieces], axis=0)


def partial_sums(acts, cot, *refs):
    pieces, out = refs[:-1], refs[-1]
    lanes = out.shape[1]
    first = is_first((BLOCK, lanes), 1)
    for b in range(pieces[0].shape[0]):
        w = matrix(pieces, b)
        proj, back = dot(rows_of(acts, b), w, NT), dot(rows_of(cot, b), w, NT)
        out[b * BLOCK:(b + 1) * BLOCK, :] = jnp.where(first, proj, SCALE * back)


def swap_matrix(lanes):
    row = lax.broadcasted_iota(jnp.int32, (lanes, lanes), 0)
    col = lax.broadcasted_iota(jnp.int32, (lanes, lanes), 1)
    return (row == jnp.where(is_first((lanes, lanes), 1), col + GROUP, col - GROUP)).astype(BF16)


def block_grads(start, acts, cot, sums, *outs):
    rows = len(outs) * 2 * GROUP
    first = is_first((rows, acts.shape[1]), 0)
    place = swap_matrix(sums.shape[1])[start * 2 * GROUP:start * 2 * GROUP + rows]
    for b in range(outs[0].shape[0]):
        q = dot(place, rows_of(sums, b), NT).astype(BF16)
        down, up = dot(q, rows_of(acts, b), NN), dot(q, rows_of(cot, b), NN)
        g = jnp.where(first, down, SCALE * up).astype(BF16)
        for i, out in enumerate(outs):
            out[b] = g[i * 2 * GROUP:(i + 1) * 2 * GROUP]


def outputs(sums, *refs):
    pieces, out, grad = refs[:-2], refs[-2], refs[-1]
    first = is_first((BLOCK, sums.shape[1]), 1)
    place = swap_matrix(sums.shape[1])
    for b in range(pieces[0].shape[0]):
        q, w = dot(rows_of(sums, b), place, NN).astype(BF16), matrix(pieces, b)
        zero = jnp.zeros_like(q)
        at = slice(b * BLOCK, (b + 1) * BLOCK)
        out[at, :] = (SCALE * dot(jnp.where(first, zero, q), w, NN)).astype(BF16)
        grad[at, :] = dot(jnp.where(first, q, zero), w, NN).astype(BF16)


def sum_pieces(nz, table, where, *refs):
    gots, (keep, send, acc) = refs[:-3], refs[-3:]
    core = where[1]
    half = keep.shape[0]
    blocks = gots[0].shape[0]
    acc[...] = jnp.zeros_like(acc)
    for step, got in zip(STEPS, gots):
        z = partner(where, nz, step)
        for b in range(blocks):
            par, row = named(table, z, core, b, blocks)
            at = par * half + row
            acc[at] = acc[at] + got[b].astype(F32)
    keep[...] = acc[pl.ds(core * half, half)]
    send[...] = acc[pl.ds((1 - core) * half, half)].astype(BF16)


def local(activations, cotangent, adapter_down_weights, adapter_up_weights, table):
    nz, nxy = lax.axis_size("z"), lax.axis_size("xy")
    share, width, rank = adapter_down_weights.shape
    tokens = activations.shape[0]
    blocks = tokens // BLOCK
    piece = (2 * GROUP, width)
    where = jnp.stack([lax.axis_index("z"), lax.axis_index("core")]).astype(jnp.int32)
    swap = [(0, 1), (1, 0)]
    own = nz * share
    slots = (shape((blocks,) + piece, BF16),) * len(STEPS)

    def over_z(x):
        return lax.all_to_all(x, "z", 0, 0, tiled=True)

    def shift(x, step):
        if step == 0:
            return x
        pairs = [(z * CORES + c, (z + (step, -step)[c]) % nz * CORES + c) for z in range(nz) for c in range(CORES)]
        return lax.ppermute(x, ("z", "core"), pairs)

    def total(part):
        rows = part.shape[0] // nxy
        got = lax.all_to_all(part.reshape(nxy, rows, part.shape[1]), "xy", 0, 0, tiled=True)
        spread = call(sum_parts, shape(got.shape, BF16), (got,), [VMEM])
        return lax.all_to_all(spread, "xy", 0, 0, tiled=True).reshape(part.shape)

    down = jnp.swapaxes(adapter_down_weights, 1, 2)
    both = [pltpu.VMEM(down.shape, BF16)] * 2 + [pltpu.SemaphoreType.DMA((2,))]
    spread = call(cut, shape((nz, share) + piece, BF16), (down, adapter_up_weights), [HBM] * 2, both)
    held = over_z(spread).reshape(own, *piece)
    held_other = lax.ppermute(held, "core", swap)
    wanted = [
        w
        for some in (FIRST, REST)
        for w in call(
            functools.partial(pick_pieces, nz, STEPS[some]), slots[some], (table, where, held, held_other),
            [SMEM, SMEM, VMEM, VMEM],
        )
    ]
    pieces = [shift(w, step) for w, step in zip(wanted, STEPS)]
    ids = (where[0] * CORES + where[1]) * share + jnp.arange(share, dtype=jnp.int32)
    counts = jnp.sum((table[:, None] == ids[None, :]).astype(F32), axis=0) * BLOCK
    pieces, counts = lax.optimization_barrier((pieces, counts))
    sums = total(
        call(
            partial_sums, shape((tokens, 2 * rank), F32), (activations, cotangent, *pieces), [VMEM] * (2 + len(STEPS))
        )
    )
    parts = [
        g
        for some in (FIRST, REST)
        for g in call(
            functools.partial(block_grads, some.start), slots[some], (activations, cotangent, sums), [VMEM] * 3
        )
    ]
    gots = [shift(g, -step) for g, step in zip(parts, STEPS)]
    out, grad = call(outputs, (shape((tokens, width), BF16),) * 2, (sums, *pieces), [VMEM] * (1 + len(STEPS)))
    gots, out, grad = lax.optimization_barrier((gots, out, grad))
    keep, send = call(
        functools.partial(sum_pieces, nz), (shape((own,) + piece, F32), shape((own,) + piece, BF16)),
        (table, where, *gots), [SMEM, SMEM] + [VMEM] * len(STEPS), [pltpu.VMEM((CORES * own,) + piece, F32)],
    )
    from_other = lax.ppermute(send, "core", swap)
    merged = call(add_other, shape((nz, share) + piece, BF16), (keep, from_other), [VMEM] * 2)
    owned = over_z(merged)
    down_grad, up_grad = call(means, (shape((share, rank, width), F32),) * 2, (counts, owned), [SMEM, VMEM])
    return out, grad, jnp.swapaxes(down_grad, 1, 2), up_grad


def solution(mesh):
    nxy = mesh.shape["adapter"]
    grid = Mesh(mesh.devices.reshape(-1, CORES, nxy), ("z", "core", "xy"))
    dp = ("z", "core")
    specs = (P(dp, "xy"), P(dp, "xy"), P(dp, "xy", None), P(dp, None, "xy"))
    return jax.shard_map(
        local, mesh=grid, in_specs=specs + (P(),), out_specs=specs, check_vma=False
    )
```

```python
import functools

import jax
import jax.numpy as jnp
from jax import lax
from jax.experimental import pallas as pl
from jax.experimental.pallas import tpu as pltpu
from jax.sharding import Mesh, PartitionSpec as P

BLOCK = 128
SCALE = 2.0
CORES = 2
COPIES = 2
GROUP = 8
STEPS = (0, 4, -3, 3, -2, 2, -1, 1)
F32, BF16 = jnp.float32, jnp.bfloat16

VMEM = pl.BlockSpec(memory_space=pltpu.VMEM)
SMEM = pl.BlockSpec(memory_space=pltpu.SMEM)
HBM = pl.BlockSpec(memory_space=pltpu.HBM)
NT = (((1,), (1,)), ((), ()))
NN = (((1,), (0,)), ((), ()))
TN = (((0,), (0,)), ((), ()))


def dot(a, b, dims):
    return lax.dot_general(a, b, dims, preferred_element_type=F32)


def call(body, outs, ins, in_specs, scratch=()):
    return pl.pallas_call(
        body,
        out_shape=outs,
        in_specs=in_specs,
        out_specs=jax.tree.map(lambda _: VMEM, outs),
        scratch_shapes=list(scratch),
        compiler_params=pltpu.CompilerParams(vmem_limit_bytes=40 * 2**20),
    )(*ins)


def shape(dims, kind):
    return jax.ShapeDtypeStruct(dims, kind)


def named(table, z, core, block, blocks):
    adapter = table[(z * CORES + core) * blocks + block]
    owner = adapter // 2
    return owner % 2, (owner // 2) * 2 + adapter % 2


def cut(down_hbm, up_hbm, out, down, up, sems):
    copies = [pltpu.make_async_copy(down_hbm, down, sems.at[0]), pltpu.make_async_copy(up_hbm, up, sems.at[1])]
    for copy in copies:
        copy.start()
    for copy in copies:
        copy.wait()
    parts = out.shape[0] // COPIES
    for k in range(down.shape[0]):
        d, u = down[k].astype(F32), up[k].astype(F32)
        for i in range(parts):
            at = slice(i * GROUP, (i + 1) * GROUP)
            piece = jnp.concatenate([d[at], u[at]], axis=0).astype(BF16)
            for copy in range(COPIES):
                out[copy * parts + i, k] = piece


def means(counts, owned, down, up):
    parts = owned.shape[0] // COPIES
    for k in range(down.shape[0]):
        for i in range(parts):
            piece = owned[i, k].astype(F32)
            for copy in range(1, COPIES):
                piece = piece + owned[copy * parts + i, k].astype(F32)
            piece = piece / counts[k]
            down[k, i * GROUP:(i + 1) * GROUP] = piece[:GROUP]
            up[k, i * GROUP:(i + 1) * GROUP] = piece[GROUP:]


def partner(where, nz, step):
    return lax.rem(where[0] + (1 - 2 * where[1]) * step + nz, nz)


def pick_pieces(nz, table, where, mine, other, *outs):
    core = where[1]
    blocks = outs[0].shape[0]
    for step, out in zip(STEPS, outs):
        z = partner(where, nz, step)
        for b in range(blocks):
            par, row = named(table, z, core, b, blocks)

            @pl.when(par == core)
            def _():
                out[b] = mine[row]

            @pl.when(par != core)
            def _():
                out[b] = other[row]


def sum_parts(got, out):
    total = got[0].astype(F32)
    for i in range(1, got.shape[0]):
        total = total + got[i].astype(F32)
    total = total.astype(BF16)
    for i in range(out.shape[0]):
        out[i] = total


def add_other(keep, other, out):
    out[...] = (keep[...] + other[...].astype(F32)).astype(BF16).reshape(out.shape)


def is_first(dims, axis):
    return lax.broadcasted_iota(jnp.int32, dims, axis) % (2 * GROUP) < GROUP


def rows_of(ref, b):
    return ref[b * BLOCK:(b + 1) * BLOCK, :]


def matrix(pieces, b):
    return jnp.concatenate([p[b] for p in pieces], axis=0)


def partial_sums(acts, cot, *refs):
    pieces, out = refs[:-1], refs[-1]
    lanes = out.shape[1]
    first = is_first((BLOCK, lanes), 1)
    for b in range(pieces[0].shape[0]):
        w = matrix(pieces, b)
        proj, back = dot(rows_of(acts, b), w, NT), dot(rows_of(cot, b), w, NT)
        out[b * BLOCK:(b + 1) * BLOCK, :] = jnp.where(first, proj, SCALE * back).astype(BF16)


def swap_matrix(lanes):
    row = lax.broadcasted_iota(jnp.int32, (lanes, lanes), 0)
    col = lax.broadcasted_iota(jnp.int32, (lanes, lanes), 1)
    return (row == jnp.where(is_first((lanes, lanes), 1), col + GROUP, col - GROUP)).astype(BF16)


def block_grads(acts, cot, sums, *outs):
    lanes = sums.shape[1]
    first = is_first((lanes, acts.shape[1]), 0)
    place = swap_matrix(lanes)
    for b in range(outs[0].shape[0]):
        q = dot(place, rows_of(sums, b), NT).astype(BF16)
        down, up = dot(q, rows_of(acts, b), NN), dot(q, rows_of(cot, b), NN)
        g = jnp.where(first, down, SCALE * up).astype(BF16)
        for i, out in enumerate(outs):
            out[b] = g[i * 2 * GROUP:(i + 1) * 2 * GROUP]


def outputs(sums, *refs):
    pieces, out, grad = refs[:-2], refs[-2], refs[-1]
    first = is_first((BLOCK, sums.shape[1]), 1)
    place = swap_matrix(sums.shape[1])
    for b in range(pieces[0].shape[0]):
        q, w = dot(rows_of(sums, b), place, NN).astype(BF16), matrix(pieces, b)
        zero = jnp.zeros_like(q)
        at = slice(b * BLOCK, (b + 1) * BLOCK)
        out[at, :] = (SCALE * dot(jnp.where(first, zero, q), w, NN)).astype(BF16)
        grad[at, :] = dot(jnp.where(first, q, zero), w, NN).astype(BF16)


def sum_pieces(nz, table, where, *refs):
    gots, (keep, send, acc) = refs[:-3], refs[-3:]
    core = where[1]
    half = keep.shape[0]
    blocks = gots[0].shape[0]
    acc[...] = jnp.zeros_like(acc)
    for step, got in zip(STEPS, gots):
        z = partner(where, nz, step)
        for b in range(blocks):
            par, row = named(table, z, core, b, blocks)
            at = par * half + row
            acc[at] = acc[at] + got[b].astype(F32)
    keep[...] = acc[pl.ds(core * half, half)]
    send[...] = acc[pl.ds((1 - core) * half, half)].astype(BF16)


def local(activations, cotangent, adapter_down_weights, adapter_up_weights, table):
    nz, nxy = lax.axis_size("z"), lax.axis_size("xy")
    share, width, rank = adapter_down_weights.shape
    tokens = activations.shape[0]
    blocks = tokens // BLOCK
    piece = (2 * GROUP, width)
    where = jnp.stack([lax.axis_index("z"), lax.axis_index("core")]).astype(jnp.int32)
    swap = [(0, 1), (1, 0)]
    own = nz * share
    slots = (shape((blocks,) + piece, BF16),) * len(STEPS)

    def over_z(x):
        return lax.all_to_all(x, "z", 0, 0, tiled=True)

    def shift(x, step):
        if step == 0:
            return x
        pairs = [(z * CORES + c, (z + (step, -step)[c]) % nz * CORES + c) for z in range(nz) for c in range(CORES)]
        return lax.ppermute(x, ("z", "core"), pairs)

    def total(part):
        rows = part.shape[0] // nxy
        got = lax.all_to_all(part.reshape(nxy, rows, part.shape[1]), "xy", 0, 0, tiled=True)
        spread = call(sum_parts, shape(got.shape, BF16), (got,), [VMEM])
        return lax.all_to_all(spread, "xy", 0, 0, tiled=True).reshape(part.shape)

    down = jnp.swapaxes(adapter_down_weights, 1, 2)
    both = [pltpu.VMEM(down.shape, BF16)] * 2 + [pltpu.SemaphoreType.DMA((2,))]
    spread = call(cut, shape((nz, share) + piece, BF16), (down, adapter_up_weights), [HBM] * 2, both)
    held = over_z(spread).reshape(own, *piece)
    held_other = lax.ppermute(held, "core", swap)
    wanted = call(
        functools.partial(pick_pieces, nz), slots, (table, where, held, held_other), [SMEM, SMEM, VMEM, VMEM]
    )
    pieces = [shift(w, step) for w, step in zip(wanted, STEPS)]
    ids = (where[0] * CORES + where[1]) * share + jnp.arange(share, dtype=jnp.int32)
    counts = jnp.sum((table[:, None] == ids[None, :]).astype(F32), axis=0) * BLOCK
    pieces, counts = lax.optimization_barrier((pieces, counts))
    sums = total(
        call(
            partial_sums, shape((tokens, 2 * rank), BF16), (activations, cotangent, *pieces), [VMEM] * (2 + len(STEPS))
        )
    )
    parts = call(block_grads, slots, (activations, cotangent, sums), [VMEM] * 3)
    gots = [shift(g, -step) for g, step in zip(parts, STEPS)]
    out, grad = call(outputs, (shape((tokens, width), BF16),) * 2, (sums, *pieces), [VMEM] * (1 + len(STEPS)))
    gots, out, grad = lax.optimization_barrier((gots, out, grad))
    keep, send = call(
        functools.partial(sum_pieces, nz), (shape((own,) + piece, F32), shape((own,) + piece, BF16)),
        (table, where, *gots), [SMEM, SMEM] + [VMEM] * len(STEPS), [pltpu.VMEM((CORES * own,) + piece, F32)],
    )
    from_other = lax.ppermute(send, "core", swap)
    merged = call(add_other, shape((nz, share) + piece, BF16), (keep, from_other), [VMEM] * 2)
    owned = over_z(merged)
    down_grad, up_grad = call(means, (shape((share, rank, width), F32),) * 2, (counts, owned), [SMEM, VMEM])
    return out, grad, jnp.swapaxes(down_grad, 1, 2), up_grad


def solution(mesh):
    nxy = mesh.shape["adapter"]
    grid = Mesh(mesh.devices.reshape(-1, CORES, nxy), ("z", "core", "xy"))
    dp = ("z", "core")
    specs = (P(dp, "xy"), P(dp, "xy"), P(dp, "xy", None), P(dp, None, "xy"))
    return jax.shard_map(
        local, mesh=grid, in_specs=specs + (P(),), out_specs=specs, check_vma=False
    )
```

```python
import functools

import jax
import jax.numpy as jnp
from jax import lax
from jax.experimental import pallas as pl
from jax.experimental.pallas import tpu as pltpu
from jax.sharding import Mesh, PartitionSpec as P

BLOCK = 128
SCALE = 2.0
CORES = 2
COPIES = 2
GROUP = 8
STEPS = (0, 4, -3, 3, -2, 2, -1, 1)
FAR = 4
F32, BF16 = jnp.float32, jnp.bfloat16

VMEM = pl.BlockSpec(memory_space=pltpu.VMEM)
SMEM = pl.BlockSpec(memory_space=pltpu.SMEM)
HBM = pl.BlockSpec(memory_space=pltpu.HBM)
NT = (((1,), (1,)), ((), ()))
NN = (((1,), (0,)), ((), ()))
TN = (((0,), (0,)), ((), ()))


def dot(a, b, dims):
    return lax.dot_general(a, b, dims, preferred_element_type=F32)


def call(body, outs, ins, in_specs, scratch=()):
    return pl.pallas_call(
        body,
        out_shape=outs,
        in_specs=in_specs,
        out_specs=jax.tree.map(lambda _: VMEM, outs),
        scratch_shapes=list(scratch),
        compiler_params=pltpu.CompilerParams(vmem_limit_bytes=40 * 2**20),
    )(*ins)


def shape(dims, kind):
    return jax.ShapeDtypeStruct(dims, kind)


def named(table, z, core, block, blocks):
    adapter = table[(z * CORES + core) * blocks + block]
    owner = adapter // 2
    return owner % 2, (owner // 2) * 2 + adapter % 2


def cut(down_hbm, up_hbm, out, down, up, sems):
    copies = [pltpu.make_async_copy(down_hbm, down, sems.at[0]), pltpu.make_async_copy(up_hbm, up, sems.at[1])]
    for copy in copies:
        copy.start()
    for copy in copies:
        copy.wait()
    parts = out.shape[0] // COPIES
    for k in range(down.shape[0]):
        d, u = down[k].astype(F32), up[k].astype(F32)
        for i in range(parts):
            at = slice(i * GROUP, (i + 1) * GROUP)
            piece = jnp.concatenate([d[at], u[at]], axis=0).astype(BF16)
            for copy in range(COPIES):
                out[copy * parts + i, k] = piece


def means(counts, owned, down, up):
    parts = owned.shape[0] // COPIES
    for k in range(down.shape[0]):
        for i in range(parts):
            piece = owned[i, k].astype(F32)
            for copy in range(1, COPIES):
                piece = piece + owned[copy * parts + i, k].astype(F32)
            piece = piece / counts[k]
            down[k, i * GROUP:(i + 1) * GROUP] = piece[:GROUP]
            up[k, i * GROUP:(i + 1) * GROUP] = piece[GROUP:]


def partner(where, nz, step):
    sign = 1 - 2 * where[1] if abs(step) == FAR else 1
    return lax.rem(where[0] + sign * step + nz, nz)


def pick_pieces(nz, table, where, mine, other, *outs):
    core = where[1]
    blocks = outs[0].shape[0]
    for step, out in zip(STEPS, outs):
        z = partner(where, nz, step)
        for b in range(blocks):
            par, row = named(table, z, core, b, blocks)

            @pl.when(par == core)
            def _():
                out[b] = mine[row]

            @pl.when(par != core)
            def _():
                out[b] = other[row]


def sum_parts(got, out):
    total = got[0]
    for i in range(1, got.shape[0]):
        total = total + got[i]
    total = total.astype(BF16)
    for i in range(out.shape[0]):
        out[i] = total


def add_other(keep, other, out):
    out[...] = (keep[...] + other[...].astype(F32)).astype(BF16).reshape(out.shape)


def is_first(dims, axis):
    return lax.broadcasted_iota(jnp.int32, dims, axis) % (2 * GROUP) < GROUP


def rows_of(ref, b):
    return ref[b * BLOCK:(b + 1) * BLOCK, :]


def matrix(pieces, b):
    return jnp.concatenate([p[b] for p in pieces], axis=0)


def partial_sums(acts, cot, *refs):
    pieces, out = refs[:-1], refs[-1]
    lanes = out.shape[1]
    first = is_first((BLOCK, lanes), 1)
    for b in range(pieces[0].shape[0]):
        w = matrix(pieces, b)
        proj, back = dot(rows_of(acts, b), w, NT), dot(rows_of(cot, b), w, NT)
        out[b * BLOCK:(b + 1) * BLOCK, :] = jnp.where(first, proj, SCALE * back)


def swap_matrix(lanes):
    row = lax.broadcasted_iota(jnp.int32, (lanes, lanes), 0)
    col = lax.broadcasted_iota(jnp.int32, (lanes, lanes), 1)
    return (row == jnp.where(is_first((lanes, lanes), 1), col + GROUP, col - GROUP)).astype(BF16)


def block_grads(acts, cot, sums, *outs):
    lanes = sums.shape[1]
    first = is_first((lanes, acts.shape[1]), 0)
    place = swap_matrix(lanes)
    for b in range(outs[0].shape[0]):
        q = dot(place, rows_of(sums, b), NT).astype(BF16)
        down, up = dot(q, rows_of(acts, b), NN), dot(q, rows_of(cot, b), NN)
        g = jnp.where(first, down, SCALE * up).astype(BF16)
        for i, out in enumerate(outs):
            out[b] = g[i * 2 * GROUP:(i + 1) * 2 * GROUP]


def outputs(sums, *refs):
    pieces, out, grad = refs[:-2], refs[-2], refs[-1]
    first = is_first((BLOCK, sums.shape[1]), 1)
    place = swap_matrix(sums.shape[1])
    for b in range(pieces[0].shape[0]):
        q, w = dot(rows_of(sums, b), place, NN).astype(BF16), matrix(pieces, b)
        zero = jnp.zeros_like(q)
        at = slice(b * BLOCK, (b + 1) * BLOCK)
        out[at, :] = (SCALE * dot(jnp.where(first, zero, q), w, NN)).astype(BF16)
        grad[at, :] = dot(jnp.where(first, q, zero), w, NN).astype(BF16)


def sum_pieces(nz, table, where, *refs):
    gots, (keep, send, acc) = refs[:-3], refs[-3:]
    core = where[1]
    half = keep.shape[0]
    blocks = gots[0].shape[0]
    acc[...] = jnp.zeros_like(acc)
    for step, got in zip(STEPS, gots):
        z = partner(where, nz, step)
        for b in range(blocks):
            par, row = named(table, z, core, b, blocks)
            at = par * half + row
            acc[at] = acc[at] + got[b].astype(F32)
    keep[...] = acc[pl.ds(core * half, half)]
    send[...] = acc[pl.ds((1 - core) * half, half)].astype(BF16)


def local(activations, cotangent, adapter_down_weights, adapter_up_weights, table):
    nz, nxy = lax.axis_size("z"), lax.axis_size("xy")
    share, width, rank = adapter_down_weights.shape
    tokens = activations.shape[0]
    blocks = tokens // BLOCK
    piece = (2 * GROUP, width)
    where = jnp.stack([lax.axis_index("z"), lax.axis_index("core")]).astype(jnp.int32)
    swap = [(0, 1), (1, 0)]
    own = nz * share
    slots = (shape((blocks,) + piece, BF16),) * len(STEPS)

    def over_z(x):
        return lax.all_to_all(x, "z", 0, 0, tiled=True)

    def shift(x, step):
        if step == 0:
            return x
        by_core = (step, -step) if abs(step) == FAR else (step, step)
        pairs = [(z * CORES + c, (z + by_core[c]) % nz * CORES + c) for z in range(nz) for c in range(CORES)]
        return lax.ppermute(x, ("z", "core"), pairs)

    def total(part):
        rows = part.shape[0] // nxy
        got = lax.all_to_all(part.reshape(nxy, rows, part.shape[1]), "xy", 0, 0, tiled=True)
        spread = call(sum_parts, shape(got.shape, BF16), (got,), [VMEM])
        return lax.all_to_all(spread, "xy", 0, 0, tiled=True).reshape(part.shape)

    down = jnp.swapaxes(adapter_down_weights, 1, 2)
    both = [pltpu.VMEM(down.shape, BF16)] * 2 + [pltpu.SemaphoreType.DMA((2,))]
    spread = call(cut, shape((nz, share) + piece, BF16), (down, adapter_up_weights), [HBM] * 2, both)
    held = over_z(spread).reshape(own, *piece)
    held_other = lax.ppermute(held, "core", swap)
    wanted = call(
        functools.partial(pick_pieces, nz), slots, (table, where, held, held_other), [SMEM, SMEM, VMEM, VMEM]
    )
    pieces = [shift(w, step) for w, step in zip(wanted, STEPS)]
    ids = (where[0] * CORES + where[1]) * share + jnp.arange(share, dtype=jnp.int32)
    counts = jnp.sum((table[:, None] == ids[None, :]).astype(F32), axis=0) * BLOCK
    pieces, counts = lax.optimization_barrier((pieces, counts))
    sums = total(
        call(
            partial_sums, shape((tokens, 2 * rank), F32), (activations, cotangent, *pieces), [VMEM] * (2 + len(STEPS))
        )
    )
    parts = call(block_grads, slots, (activations, cotangent, sums), [VMEM] * 3)
    gots = [shift(g, -step) for g, step in zip(parts, STEPS)]
    out, grad = call(outputs, (shape((tokens, width), BF16),) * 2, (sums, *pieces), [VMEM] * (1 + len(STEPS)))
    gots, out, grad = lax.optimization_barrier((gots, out, grad))
    keep, send = call(
        functools.partial(sum_pieces, nz), (shape((own,) + piece, F32), shape((own,) + piece, BF16)),
        (table, where, *gots), [SMEM, SMEM] + [VMEM] * len(STEPS), [pltpu.VMEM((CORES * own,) + piece, F32)],
    )
    from_other = lax.ppermute(send, "core", swap)
    merged = call(add_other, shape((nz, share) + piece, BF16), (keep, from_other), [VMEM] * 2)
    owned = over_z(merged)
    down_grad, up_grad = call(means, (shape((share, rank, width), F32),) * 2, (counts, owned), [SMEM, VMEM])
    return out, grad, jnp.swapaxes(down_grad, 1, 2), up_grad


def solution(mesh):
    nxy = mesh.shape["adapter"]
    grid = Mesh(mesh.devices.reshape(-1, CORES, nxy), ("z", "core", "xy"))
    dp = ("z", "core")
    specs = (P(dp, "xy"), P(dp, "xy"), P(dp, "xy", None), P(dp, None, "xy"))
    return jax.shard_map(
        local, mesh=grid, in_specs=specs + (P(),), out_specs=specs, check_vma=False
    )
```
